32 devices in a mesh: expert: 32 (over z, y, x, core), tensor: 1.
Axes of the slice: x: 2, y: 2, z: 4, core: 2. Of those that a mesh axis runs over, the one named last changes fastest.
Arguments:
- tokens: bfloat16 [8192, 2048], P('expert', 'tensor'), may hold values from -6 to 6
- out_grads: bfloat16 [8192, 2048], P('expert', 'tensor'), may hold values from -6 to 6
- species: int32 [8192, 1], P('expert'), may hold values from 0 to 31; in each aligned block of 256 rows (0 to 255, 256 to 511, ...) at most 16 rows name the same one
- expert_table: int32 [32], replicated, may hold values from 0 to 31, each once
- gate_weight: bfloat16 [32, 2048, 4096], P('expert', None, 'tensor'), may hold values from -0.125 to 0.125
- up_weight: bfloat16 [32, 2048, 4096], P('expert', None, 'tensor'), may hold values from -0.125 to 0.125
- down_weight: bfloat16 [32, 4096, 2048], P('expert', 'tensor'), may hold values from -0.09375 to 0.09375
Outputs:
- token_grads: bfloat16 [8192, 2048], P('expert', 'tensor')
The draws below stay inside these ranges and needn't reach their ends.
Inputs may be any that keep to these rules, and one draw needn't show every extreme that they name: In each aligned block of 256 rows no species occurs more than 16 times, and in some blocks one species occurs exactly 16 times. `expert_table`: each species has a different expert.
All inputs are finite; a program needn't handle non-finite values.
Results may differ from the reference program's by a relative error of at most 0.0095.
Values may be sent and summed in bfloat16 or wider, within the bound.
No kernel may reach another device: no remote copies, remote signals or barrier semaphores. Data moves between devices by JAX's collectives and lax.ppermute only.
A program may use at most 128 MiB of HBM per device.

```python
import math
import jax
import jax.numpy as jnp
import numpy as np
from jax import lax

D = 2048
FF = 4096
EXPERTS = 32
TOKENS = 8192
ROWS_DEV = 256
FF_DEV = 4096
CAP = 16
SLOTS = 512
N_TENSOR = 1


def block_levels(rng, shape, pieces, low, high):
    def one(dim, parts):
        steps = jax.random.uniform(jax.random.fold_in(jax.random.fold_in(rng, 6), dim), (parts,), jnp.float32, low / len(pieces), high / len(pieces))
        return jnp.repeat(jnp.exp(steps), shape[dim] // parts).reshape((-1,) + (1,) * (len(shape) - dim - 1))

    factor_of = one(*pieces[0])
    for cut in pieces[1:]:
        factor_of = factor_of * one(*cut)
    return factor_of


def assign_block(rng, own, number, rows, number_of, top, most, lean):
    order = jax.random.permutation(rng, number_of)
    crowded, ordinary = shares(number_of, rows * top, most, lean, True), shares(number_of, rows * top, most, lean, False)
    places = jnp.arange(number_of)

    def named(sizes, rotation):
        used = int((sizes > 0).sum())
        fixed = max(1, used // 4)
        passed = fixed + (places - fixed + rotation * (used - fixed)) % max(1, number_of - fixed)
        return jnp.zeros((number_of,), jnp.int32).at[order[jnp.where(places < fixed, places, passed)]].set(jnp.asarray(sizes, jnp.int32))

    sizes = jnp.where(number % 4 == 0, named(crowded, number // 4), named(ordinary, number - number // 4 - 1))
    mixed = jax.random.permutation(jax.random.fold_in(own, 3), number_of)
    source_of, receiver = mixed[0:number_of // 2 * 2:2], mixed[1:number_of // 2 * 2:2]
    margin = jnp.minimum(sizes[source_of] - 1, most - sizes[receiver]) // 2
    margin = jnp.where((source_of == order[0]) | (receiver == order[0]) | (sizes[receiver] == 0), 0, jnp.maximum(margin, 0))
    passed = jax.random.randint(jax.random.fold_in(own, 4), (number_of // 2,), 0, 1 << 20) % (margin + 1)
    sizes = sizes.at[source_of].add(-passed).at[receiver].add(passed)
    items = jnp.searchsorted(jnp.cumsum(sizes), jnp.arange(rows * top), side="right").astype(jnp.int32)
    listing = items.reshape(top, rows).T
    listing = listing[jax.random.permutation(jax.random.fold_in(own, 1), rows)]
    rotation = jax.random.randint(jax.random.fold_in(own, 2), (rows, 1), 0, top)
    return jnp.take_along_axis(listing, (jnp.arange(top)[None, :] + rotation) % top, axis=1)


def shares(number_of, total, most, slope, full):
    loads = [(1 << 20) // math.isqrt(rank ** slope) + 1 for rank in range(1, number_of + 1)]
    largest = most if full else min(most, max(-(-total // number_of), total * loads[0] // sum(loads)))
    least = 1 if total - largest >= number_of - 1 else 0
    holding, rest = [largest] + [least] * (number_of - 1), total - largest - least * (number_of - 1)
    while rest > 0:
        candidates = [i for i in range(1, number_of) if holding[i] < largest] or [i for i in range(1, number_of) if holding[i] < most]
        pool, left = sum([loads[i] for i in candidates]), rest
        for i in candidates:
            more = min(most - holding[i], max(1, left * loads[i] // pool), rest)
            holding[i] = holding[i] + more
            rest = rest - more
    return np.array(holding)


def bell_draw(own_key, extent, width, reach, split=(), kind=jnp.bfloat16):
    result = jax.random.normal(own_key, extent, jnp.float32) * width
    if len(split) > 0:
        result = block_levels(own_key, extent, split, -0.22, 0.18) * result
    return jnp.clip(result, min=-reach, max=reach).astype(kind)


def setup_inputs(seed: int = 0) -> dict:
    seeds = jax.random.split(jax.random.key(seed), 8)
    tokens = bell_draw(seeds[0], (TOKENS, D), 1.0, 6.0, ((0, 32),))
    out_grads = bell_draw(seeds[1], (TOKENS, D), 1.0, 6.0, ((0, 32),))
    species_keys = jax.random.split(jax.random.fold_in(seeds[2], 1), TOKENS // ROWS_DEV)
    species_turns = jax.random.permutation(jax.random.fold_in(seeds[2], 3), TOKENS // ROWS_DEV)
    species = jax.vmap(lambda own, number: assign_block(jax.random.fold_in(seeds[2], 2), own, number, ROWS_DEV, EXPERTS, 1, CAP, 2))(species_keys, species_turns).reshape((TOKENS, 1))
    expert_table = jax.random.permutation(seeds[3], EXPERTS).astype(jnp.int32)
    gate_weight = bell_draw(seeds[4], (EXPERTS, D, FF), D ** -0.5, 0.125, ((0, 32),))
    up_weight = bell_draw(seeds[5], (EXPERTS, D, FF), D ** -0.5, 0.125, ((0, 32),))
    down_weight = bell_draw(seeds[6], (EXPERTS, FF, D), FF ** -0.5, 0.09375, ((0, 32),))
    return dict(tokens=tokens, out_grads=out_grads, species=species, expert_table=expert_table, gate_weight=gate_weight, up_weight=up_weight, down_weight=down_weight)


def slot_positions(species, expert_table):
    expert_of = expert_table[species[:, 0]].astype(jnp.int32)
    blocked = expert_of.reshape(-1, ROWS_DEV)
    expert_ids = jnp.arange(EXPERTS, dtype=jnp.int32)
    onehot = (blocked[:, :, None] == expert_ids[None, None, :]).astype(jnp.int32)
    earlier = jnp.cumsum(onehot, axis=1) - onehot
    slot_of = jnp.sum(earlier * onehot, axis=2)
    block_ids = jnp.arange(blocked.shape[0], dtype=jnp.int32)[:, None]
    position = blocked * SLOTS + block_ids * CAP + slot_of
    return position.reshape(-1).astype(jnp.int32)


def expert_pass(expert_rows, expert_grads, gate_matrix, up_matrix, down_matrix):
    contract = (((1,), (1,)), ((), ()))
    gate_pre = jnp.dot(expert_rows, gate_matrix, preferred_element_type=jnp.float32)
    up_pre = jnp.dot(expert_rows, up_matrix, preferred_element_type=jnp.float32)
    hidden_grad = lax.dot_general(expert_grads, down_matrix, contract, preferred_element_type=jnp.float32)
    sigmoid_gate = jax.nn.sigmoid(gate_pre)
    up_grad = (hidden_grad * gate_pre * sigmoid_gate).astype(jnp.bfloat16)
    gate_grad = (hidden_grad * up_pre * sigmoid_gate * (1.0 + gate_pre * (1.0 - sigmoid_gate))).astype(jnp.bfloat16)
    running = jnp.zeros((expert_rows.shape[0], D), jnp.float32)
    for block_index in range(N_TENSOR):
        start = block_index * FF_DEV
        partial_sum = lax.dot_general(gate_grad[:, start:start + FF_DEV], gate_matrix[:, start:start + FF_DEV], contract, preferred_element_type=jnp.float32)
        partial_sum = partial_sum + lax.dot_general(up_grad[:, start:start + FF_DEV], up_matrix[:, start:start + FF_DEV], contract, preferred_element_type=jnp.float32)
        rounded = lax.optimization_barrier(partial_sum.astype(jnp.bfloat16))
        running = running + rounded.astype(jnp.float32)
    return running.astype(jnp.bfloat16)


def reference(tokens, out_grads, species, expert_table, gate_weight, up_weight, down_weight):
    position = slot_positions(species, expert_table)
    owner_rows = jnp.full((EXPERTS * SLOTS,), TOKENS, jnp.int32)
    owner_rows = owner_rows.at[position].set(jnp.arange(TOKENS, dtype=jnp.int32))
    owner_rows = owner_rows.reshape(EXPERTS, SLOTS)
    padded_rows = jnp.concatenate([tokens, jnp.zeros((1, D), jnp.bfloat16)], axis=0)
    padded_grads = jnp.concatenate([out_grads, jnp.zeros((1, D), jnp.bfloat16)], axis=0)

    def per_expert(expert_index):
        picked = owner_rows[expert_index]
        return expert_pass(padded_rows[picked], padded_grads[picked], gate_weight[expert_index], up_weight[expert_index], down_weight[expert_index])

    row_grads = lax.map(per_expert, jnp.arange(EXPERTS, dtype=jnp.int32))
    return row_grads.reshape(EXPERTS * SLOTS, D)[position]
```

```python
import jax
import jax.numpy as jnp
from jax import lax
from jax.sharding import PartitionSpec as P

PIECES = 2


def dot(a, b, contract):
    return lax.dot_general(a, b, (contract, ((), ())), preferred_element_type=jnp.float32)


def expert_partial(gate_pre, up_pre, hidden_grad, gate_matrix, up_matrix):
    sigmoid_gate = jax.nn.sigmoid(gate_pre)
    up_grad = (hidden_grad * gate_pre * sigmoid_gate).astype(jnp.bfloat16)
    gate_grad = (
        hidden_grad * up_pre * sigmoid_gate * (1.0 + gate_pre * (1.0 - sigmoid_gate))
    ).astype(jnp.bfloat16)
    return dot(gate_grad, gate_matrix, ((1,), (1,))) + dot(up_grad, up_matrix, ((1,), (1,)))


def places(species, expert_table, tensor_size, capacity):
    experts = expert_table.shape[0]
    rows_dev = species.shape[0] // tensor_size
    expert_ids = jnp.arange(experts, dtype=jnp.int32)
    species_hits = species == expert_ids[None, :]
    expert_of = jnp.sum(jnp.where(species_hits, expert_table[None, :], 0), axis=1).reshape(
        tensor_size, rows_dev
    )
    onehot = (expert_of[:, :, None] == expert_ids[None, None, :]).astype(jnp.int32)
    earlier = jnp.cumsum(onehot, axis=1) - onehot
    slot_of = jnp.sum(earlier * onehot, axis=2)
    return expert_of, slot_of


def per_device(tokens, out_grads, species, expert_table, gate_weight, up_weight, down_weight):
    tensor_size = lax.axis_size("tensor")
    tensor_index = lax.axis_index("tensor")
    experts = expert_table.shape[0]
    rows_dev = tokens.shape[0] // tensor_size
    model_width = tokens.shape[1] * tensor_size
    capacity = 2 * rows_dev // experts
    pieces = PIECES if capacity % (8 * PIECES) == 0 else 1
    depth = capacity // pieces
    expert_of, slot_of = places(species, expert_table, tensor_size, capacity)
    gate, up, down = gate_weight[0], up_weight[0], down_weight[0]
    group_tokens, group_grads = (
        lax.all_gather(tokens, "tensor", axis=1, tiled=True),
        lax.all_gather(out_grads, "tensor", axis=1, tiled=True),
    )
    place_ids = jnp.arange(experts * depth, dtype=jnp.int32)

    def select_of(piece):
        slot = slot_of - piece * depth
        place = jnp.where((slot >= 0) & (slot < depth), expert_of * depth + slot, -1)
        return (place_ids[None, :, None] == place[:, None, :]).astype(jnp.bfloat16)

    def send(select, rows):
        packed = jnp.einsum(
            "tecr,trd->etcd",
            select.reshape(tensor_size, experts, depth, rows_dev),
            rows.reshape(tensor_size, rows_dev, model_width),
            preferred_element_type=jnp.float32,
        ).astype(jnp.bfloat16)
        packed = packed.reshape(experts, tensor_size * depth, model_width)
        return lax.all_to_all(packed, "expert", split_axis=0, concat_axis=0, tiled=True)

    selects = [select_of(k) for k in range(pieces)]
    arrived = [(send(s, group_tokens), send(s, group_grads)) for s in selects]
    own = None
    for select, (rows, grads) in zip(selects, arrived):
        slot_count = rows.shape[0] * rows.shape[1]
        rows = rows.reshape(slot_count, model_width)
        grads = grads.reshape(slot_count, model_width)
        gate_pre = dot(rows, gate, ((1,), (0,)))
        up_pre = dot(rows, up, ((1,), (0,)))
        hidden_grad = dot(grads, down, ((1,), (1,)))
        partial_sum = expert_partial(gate_pre, up_pre, hidden_grad, gate, up)
        summed = lax.psum_scatter(
            partial_sum.reshape(experts, tensor_size * depth, model_width).astype(jnp.bfloat16),
            "tensor",
            scatter_dimension=1,
            tiled=True,
        )
        returned = lax.all_to_all(summed, "expert", split_axis=0, concat_axis=0, tiled=True)
        own_select = lax.dynamic_index_in_dim(select, tensor_index, 0, keepdims=False)
        term = dot(own_select, returned.reshape(experts * depth, model_width), ((0,), (0,)))
        own = term if own is None else own + term
    return lax.all_to_all(
        own.astype(jnp.bfloat16), "tensor", split_axis=1, concat_axis=0, tiled=True
    )


def solution(mesh):
    placed = (
        P("expert", "tensor"),
        P("expert", "tensor"),
        P("expert", None),
        P(),
        P("expert", None, "tensor"),
        P("expert", None, "tensor"),
        P("expert", "tensor", None),
    )
    return jax.shard_map(
        per_device, mesh=mesh, in_specs=placed, out_specs=P("expert", "tensor"), check_vma=False
    )
```

```python
import functools

import jax
import jax.numpy as jnp
from jax import lax
from jax.experimental import pallas as pl
from jax.experimental.pallas import tpu as pltpu
from jax.sharding import PartitionSpec as P

PIECES = 2
MIB = 1 << 20


def dot(a, b, contract):
    return lax.dot_general(a, b, (contract, ((), ())), preferred_element_type=jnp.float32)


def hidden_grads(gate_pre, up_pre, hidden_grad):
    sigmoid_gate = jax.nn.sigmoid(gate_pre)
    up_grad = (hidden_grad * gate_pre * sigmoid_gate).astype(jnp.bfloat16)
    gate_grad = (
        hidden_grad * up_pre * sigmoid_gate * (1.0 + gate_pre * (1.0 - sigmoid_gate))
    ).astype(jnp.bfloat16)
    return gate_grad, up_grad


def expert_partial(rows, grads, gate, up, down):
    gate_pre, up_pre = dot(rows, gate, ((1,), (0,))), dot(rows, up, ((1,), (0,)))
    hidden_grad = dot(grads, down, ((1,), (1,)))
    gate_grad, up_grad = hidden_grads(gate_pre, up_pre, hidden_grad)
    partial_sum = dot(gate_grad, gate, ((1,), (1,))) + dot(up_grad, up, ((1,), (1,)))
    return partial_sum.astype(jnp.bfloat16)


def expert_kernel(pair_ref, gate_ref, up_ref, down_ref, out_ref, total):
    width = out_ref.shape[1]
    step = pl.program_id(0)

    @pl.when(step == 0)
    def _():
        total[...] = jnp.zeros_like(total)

    gate, up = gate_ref[0], up_ref[0]
    rows = pair_ref[:, :width]
    gate_pre, up_pre = dot(rows, gate, ((1,), (0,))), dot(rows, up, ((1,), (0,)))
    hidden_grad = dot(pair_ref[:, width:], down_ref[0], ((1,), (1,)))
    gate_grad, up_grad = hidden_grads(gate_pre, up_pre, hidden_grad)
    total[...] += dot(gate_grad, gate, ((1,), (1,))) + dot(up_grad, up, ((1,), (1,)))

    @pl.when(step == pl.num_programs(0) - 1)
    def _():
        out_ref[...] = total[...].astype(out_ref.dtype)


def expert_piece(pair, gate_weight, up_weight, down_weight):
    rows, width = pair.shape[0], pair.shape[1] // 2
    hidden = gate_weight.shape[2]
    tile = min(512, hidden)
    return pl.pallas_call(
        expert_kernel,
        grid=(hidden // tile,),
        in_specs=[
            pl.BlockSpec((rows, 2 * width), lambda i: (0, 0)),
            pl.BlockSpec((1, width, tile), lambda i: (0, 0, i)),
            pl.BlockSpec((1, width, tile), lambda i: (0, 0, i)),
            pl.BlockSpec((1, tile, width), lambda i: (0, i, 0)),
        ],
        out_specs=pl.BlockSpec((rows, width), lambda i: (0, 0)),
        out_shape=jax.ShapeDtypeStruct((rows, width), jnp.bfloat16),
        scratch_shapes=[pltpu.VMEM((rows, width), jnp.float32)],
        compiler_params=pltpu.CompilerParams(vmem_limit_bytes=40 * MIB),
        cost_estimate=pl.CostEstimate(
            flops=10 * rows * width * hidden,
            bytes_accessed=6 * width * hidden + 6 * rows * width,
            transcendentals=rows * hidden,
        ),
    )(pair, gate_weight, up_weight, down_weight)


def pack_kernel(place_ref, rows_ref, grads_ref, out_ref):
    count, width = out_ref.shape[0], rows_ref.shape[1]
    ids = lax.broadcasted_iota(jnp.int32, (count, place_ref.shape[1]), 0)
    select = (ids == place_ref[...]).astype(jnp.bfloat16)
    out_ref[:, :width] = dot(select, rows_ref[...], ((1,), (0,))).astype(out_ref.dtype)
    out_ref[:, width:] = dot(select, grads_ref[...], ((1,), (0,))).astype(out_ref.dtype)


def pack_pair(place, tokens, out_grads, count):
    rows, width = tokens.shape
    return pl.pallas_call(
        pack_kernel,
        out_shape=jax.ShapeDtypeStruct((count, 2 * width), jnp.bfloat16),
        compiler_params=pltpu.CompilerParams(vmem_limit_bytes=24 * MIB),
        cost_estimate=pl.CostEstimate(
            flops=4 * count * rows * width, bytes_accessed=4 * (rows + count) * width, transcendentals=0
        ),
    )(place[None, :], tokens, out_grads)


def places(species, expert_table, tensor_size):
    experts = expert_table.shape[0]
    rows_dev = species.shape[0] // tensor_size
    expert_ids = jnp.arange(experts, dtype=jnp.int32)
    species_hits = species == expert_ids[None, :]
    expert_of = jnp.sum(jnp.where(species_hits, expert_table[None, :], 0), axis=1).reshape(
        tensor_size, rows_dev
    )
    onehot = (expert_of[:, :, None] == expert_ids[None, None, :]).astype(jnp.int32)
    earlier = jnp.cumsum(onehot, axis=1) - onehot
    slot_of = jnp.sum(earlier * onehot, axis=2)
    return expert_of, slot_of


def in_pieces(tokens, out_grads, species, expert_table, gate_weight, up_weight, down_weight):
    rows_dev, width = tokens.shape
    experts = expert_table.shape[0]
    depth = 2 * rows_dev // experts // PIECES
    count = experts * depth
    expert_of, slot_of = places(species, expert_table, 1)
    slot = slot_of[0][None, :] - depth * jnp.arange(PIECES, dtype=jnp.int32)[:, None]
    place_of = jnp.where((slot >= 0) & (slot < depth), expert_of * depth + slot, -1)
    exchange = functools.partial(
        lax.all_to_all, axis_name="expert", split_axis=0, concat_axis=0, tiled=True
    )
    arrived = []
    for piece in range(PIECES):
        packed = pack_pair(place_of[piece], tokens, out_grads, count)
        arrived.append(exchange(packed.reshape(experts, depth, 2 * width)))
    own = None
    for piece in range(PIECES):
        pair = arrived[piece].reshape(count, 2 * width)
        partial_sum = expert_piece(pair, gate_weight, up_weight, down_weight)
        returned = exchange(partial_sum.reshape(experts, depth, width)).reshape(count, width)
        ids = jnp.arange(count, dtype=jnp.int32)
        select = (ids[:, None] == place_of[piece][None, :]).astype(jnp.bfloat16)
        term = dot(select, returned, ((0,), (0,)))
        own = term if own is None else own + term
    return own.astype(jnp.bfloat16)


def in_groups(tokens, out_grads, species, expert_table, gate_weight, up_weight, down_weight):
    tensor_size = lax.axis_size("tensor")
    tensor_index = lax.axis_index("tensor")
    experts = expert_table.shape[0]
    rows_dev = tokens.shape[0] // tensor_size
    model_width = tokens.shape[1] * tensor_size
    capacity = 2 * rows_dev // experts
    expert_of, slot_of = places(species, expert_table, tensor_size)
    group_tokens, group_grads = (
        lax.all_gather(tokens, "tensor", axis=1, tiled=True),
        lax.all_gather(out_grads, "tensor", axis=1, tiled=True),
    )
    place_of = expert_of * capacity + slot_of
    place_ids = jnp.arange(experts * capacity, dtype=jnp.int32)
    select = (place_ids[None, :, None] == place_of[:, None, :]).astype(jnp.bfloat16)

    def send(rows):
        packed = jnp.einsum(
            "tecr,trd->etcd",
            select.reshape(tensor_size, experts, capacity, rows_dev),
            rows.reshape(tensor_size, rows_dev, model_width),
            preferred_element_type=jnp.float32,
        ).astype(jnp.bfloat16)
        packed = packed.reshape(experts, tensor_size * capacity, model_width)
        arrived = lax.all_to_all(packed, "expert", split_axis=0, concat_axis=0, tiled=True)
        return arrived.reshape(-1, model_width)

    partial_sum = expert_partial(
        send(group_tokens), send(group_grads), gate_weight[0], up_weight[0], down_weight[0]
    )
    summed = lax.psum_scatter(
        partial_sum.reshape(experts, tensor_size * capacity, model_width),
        "tensor",
        scatter_dimension=1,
        tiled=True,
    )
    returned = lax.all_to_all(summed, "expert", split_axis=0, concat_axis=0, tiled=True)
    own_select = lax.dynamic_index_in_dim(select, tensor_index, 0, keepdims=False)
    own = dot(own_select, returned.reshape(experts * capacity, model_width), ((0,), (0,)))
    return lax.all_to_all(
        own.astype(jnp.bfloat16), "tensor", split_axis=1, concat_axis=0, tiled=True
    )


def per_device(tokens, out_grads, species, expert_table, *weights):
    whole = lax.axis_size("tensor") == 1
    capacity = 2 * tokens.shape[0] // expert_table.shape[0]
    form = in_pieces if whole and capacity % (8 * PIECES) == 0 else in_groups
    return form(tokens, out_grads, species, expert_table, *weights)


def solution(mesh):
    placed = (
        P("expert", "tensor"),
        P("expert", "tensor"),
        P("expert", None),
        P(),
        P("expert", None, "tensor"),
        P("expert", None, "tensor"),
        P("expert", "tensor", None),
    )
    return jax.shard_map(
        per_device, mesh=mesh, in_specs=placed, out_specs=P("expert", "tensor"), check_vma=False
    )
```

```python
import jax
import jax.numpy as jnp
from jax import lax
from jax.experimental import pallas as pl
from jax.experimental.pallas import tpu as pltpu
from jax.sharding import PartitionSpec as P

MIB = 1 << 20


def dot(a, b, contract):
    return lax.dot_general(a, b, (contract, ((), ())), preferred_element_type=jnp.float32)


def hidden_grads(gate_pre, up_pre, hidden_grad):
    sigmoid_gate = jax.nn.sigmoid(gate_pre)
    up_grad = (hidden_grad * gate_pre * sigmoid_gate).astype(jnp.bfloat16)
    gate_grad = (
        hidden_grad * up_pre * sigmoid_gate * (1.0 + gate_pre * (1.0 - sigmoid_gate))
    ).astype(jnp.bfloat16)
    return gate_grad, up_grad


def expert_partial(rows, grads, gate, up, down):
    gate_pre, up_pre = dot(rows, gate, ((1,), (0,))), dot(rows, up, ((1,), (0,)))
    hidden_grad = dot(grads, down, ((1,), (1,)))
    gate_grad, up_grad = hidden_grads(gate_pre, up_pre, hidden_grad)
    partial_sum = dot(gate_grad, gate, ((1,), (1,))) + dot(up_grad, up, ((1,), (1,)))
    return partial_sum.astype(jnp.bfloat16)


def expert_kernel(*refs):
    count = (len(refs) - 5) // 2
    block_refs, (gate_ref, up_ref, down_ref) = refs[:count], refs[count : count + 3]
    out_refs, (pair, total) = refs[count + 3 : 2 * count + 3], refs[2 * count + 3 :]
    depth, width = out_refs[0].shape
    step = pl.program_id(0)

    @pl.when(step == 0)
    def _():
        for k, block_ref in enumerate(block_refs):
            pair[k * depth : (k + 1) * depth, :] = block_ref[...]
        total[...] = jnp.zeros_like(total)

    gate, up = gate_ref[0], up_ref[0]
    rows = pair[:, :width]
    gate_pre, up_pre = dot(rows, gate, ((1,), (0,))), dot(rows, up, ((1,), (0,)))
    hidden_grad = dot(pair[:, width:], down_ref[0], ((1,), (1,)))
    gate_grad, up_grad = hidden_grads(gate_pre, up_pre, hidden_grad)
    total[...] += dot(gate_grad, gate, ((1,), (1,))) + dot(up_grad, up, ((1,), (1,)))

    @pl.when(step == pl.num_programs(0) - 1)
    def _():
        for k, out_ref in enumerate(out_refs):
            out_ref[...] = total[k * depth : (k + 1) * depth, :].astype(out_ref.dtype)


def expert_piece(blocks, gate_weight, up_weight, down_weight):
    depth, width = blocks[0].shape[0], blocks[0].shape[1] // 2
    rows = depth * len(blocks)
    hidden = gate_weight.shape[2]
    tile = min(512, hidden)
    return pl.pallas_call(
        expert_kernel,
        grid=(hidden // tile,),
        in_specs=[pl.BlockSpec((depth, 2 * width), lambda i: (0, 0))] * len(blocks)
        + [
            pl.BlockSpec((1, width, tile), lambda i: (0, 0, i)),
            pl.BlockSpec((1, width, tile), lambda i: (0, 0, i)),
            pl.BlockSpec((1, tile, width), lambda i: (0, i, 0)),
        ],
        out_specs=[pl.BlockSpec((depth, width), lambda i: (0, 0))] * len(blocks),
        out_shape=[jax.ShapeDtypeStruct((depth, width), jnp.bfloat16)] * len(blocks),
        scratch_shapes=[
            pltpu.VMEM((rows, 2 * width), jnp.bfloat16),
            pltpu.VMEM((rows, width), jnp.float32),
        ],
        compiler_params=pltpu.CompilerParams(vmem_limit_bytes=40 * MIB),
        cost_estimate=pl.CostEstimate(
            flops=10 * rows * width * hidden,
            bytes_accessed=6 * width * hidden + 6 * rows * width,
            transcendentals=rows * hidden,
        ),
        name="expert_piece",
    )(*blocks, gate_weight, up_weight, down_weight)


def pack_kernel(place_ref, rows_ref, grads_ref, *out_refs):
    depth, width = out_refs[0].shape[0], rows_ref.shape[1]
    count = depth * len(out_refs)
    ids = lax.broadcasted_iota(jnp.int32, (count, place_ref.shape[1]), 0)
    select = (ids == place_ref[...]).astype(jnp.bfloat16)
    for low, ref in ((0, rows_ref), (width, grads_ref)):
        packed = dot(select, ref[...], ((1,), (0,))).astype(jnp.bfloat16)
        for k, out_ref in enumerate(out_refs):
            out_ref[:, low : low + width] = packed[k * depth : (k + 1) * depth, :]


def pack_blocks(place, tokens, out_grads, blocks, depth):
    rows, width = tokens.shape
    count = blocks * depth
    return pl.pallas_call(
        pack_kernel,
        out_shape=[jax.ShapeDtypeStruct((depth, 2 * width), jnp.bfloat16)] * blocks,
        compiler_params=pltpu.CompilerParams(vmem_limit_bytes=24 * MIB),
        cost_estimate=pl.CostEstimate(
            flops=4 * count * rows * width, bytes_accessed=4 * (rows + count) * width, transcendentals=0
        ),
        name="pack_blocks",
    )(place[None, :], tokens, out_grads)


def unpack_kernel(*refs):
    (place_ref, before_ref), (out_ref, gathered) = refs[:2], refs[-2:]
    low = 0
    for block_ref in refs[2:-2]:
        high = low + block_ref.shape[0]
        gathered[low:high, :] = block_ref[...]
        low = high
    ids = lax.broadcasted_iota(jnp.int32, (place_ref.shape[0], low), 1)
    select = (ids == place_ref[...]).astype(jnp.bfloat16)
    found = dot(select, gathered[...], ((1,), (0,)))
    out_ref[...] = (found + before_ref[...].astype(jnp.float32)).astype(out_ref.dtype)


def unpack_blocks(place, before, blocks):
    rows, width = before.shape
    count = sum(block.shape[0] for block in blocks)
    return pl.pallas_call(
        unpack_kernel,
        out_shape=jax.ShapeDtypeStruct((rows, width), jnp.bfloat16),
        scratch_shapes=[pltpu.VMEM((count, width), jnp.bfloat16)],
        compiler_params=pltpu.CompilerParams(vmem_limit_bytes=24 * MIB),
        cost_estimate=pl.CostEstimate(
            flops=2 * rows * count * width,
            bytes_accessed=2 * (2 * rows + count) * width,
            transcendentals=0,
        ),
        name="unpack_blocks",
    )(place[:, None], before, *blocks)


def places(species, expert_table, tensor_size):
    experts = expert_table.shape[0]
    rows_dev = species.shape[0] // tensor_size
    expert_ids = jnp.arange(experts, dtype=jnp.int32)
    species_hits = species == expert_ids[None, :]
    expert_of = jnp.sum(jnp.where(species_hits, expert_table[None, :], 0), axis=1).reshape(
        tensor_size, rows_dev
    )
    onehot = (expert_of[:, :, None] == expert_ids[None, None, :]).astype(jnp.int32)
    earlier = jnp.cumsum(onehot, axis=1) - onehot
    slot_of = jnp.sum(earlier * onehot, axis=2)
    return expert_of, slot_of


def after(arrays, others):
    tied = lax.optimization_barrier((tuple(arrays), tuple(others)))
    return list(tied[0])


def in_halves(tokens, out_grads, species, expert_table, gate_weight, up_weight, down_weight):
    rows_dev, width = tokens.shape
    experts = expert_table.shape[0]
    depth, half = 2 * rows_dev // experts, experts // 2
    count = half * depth
    expert_of, slot_of = (found[0] for found in places(species, expert_table, 1))
    step_of = expert_of ^ lax.axis_index("expert").astype(jnp.int32)
    far_place = jnp.where(step_of >= half, (step_of - half) * depth + slot_of, -1)
    near_place = jnp.where(step_of < half, (expert_of % half) * depth + slot_of, -1)
    weights = gate_weight, up_weight, down_weight

    def hop(array, k):
        return lax.ppermute(array, "expert", [(i, i ^ (half + k)) for i in range(experts)])

    def exchange(array):
        return lax.all_to_all(
            array.reshape(half, depth, -1),
            "expert",
            split_axis=0,
            concat_axis=0,
            axis_index_groups=[list(range(half)), list(range(half, experts))],
            tiled=True,
        ).reshape(count, -1)

    far = pack_blocks(far_place, tokens, out_grads, half, depth)
    far = [hop(block, k) for k, block in enumerate(far)]
    near = exchange(pack_blocks(near_place, tokens, out_grads, 1, count)[0])
    near = exchange(expert_piece([near], *weights)[0])
    split = half // 2
    first = expert_piece(far[:split], *weights)
    first = [hop(block, k) for k, block in enumerate(after(first, far[split:]))]
    last = expert_piece(far[split:], *weights)
    last = [hop(block, k + split) for k, block in enumerate(last)]
    own = unpack_blocks(near_place, jnp.zeros_like(tokens), [near])
    first_place = jnp.where(far_place < split * depth, far_place, -1)
    own = unpack_blocks(first_place, own, first)
    return unpack_blocks(far_place - split * depth, own, last)


def in_groups(tokens, out_grads, species, expert_table, gate_weight, up_weight, down_weight):
    tensor_size = lax.axis_size("tensor")
    tensor_index = lax.axis_index("tensor")
    experts = expert_table.shape[0]
    rows_dev = tokens.shape[0] // tensor_size
    model_width = tokens.shape[1] * tensor_size
    capacity = 2 * rows_dev // experts
    expert_of, slot_of = places(species, expert_table, tensor_size)
    group_tokens, group_grads = (
        lax.all_gather(tokens, "tensor", axis=1, tiled=True),
        lax.all_gather(out_grads, "tensor", axis=1, tiled=True),
    )
    place_of = expert_of * capacity + slot_of
    place_ids = jnp.arange(experts * capacity, dtype=jnp.int32)
    select = (place_ids[None, :, None] == place_of[:, None, :]).astype(jnp.bfloat16)

    def send(rows):
        packed = jnp.einsum(
            "tecr,trd->etcd",
            select.reshape(tensor_size, experts, capacity, rows_dev),
            rows.reshape(tensor_size, rows_dev, model_width),
            preferred_element_type=jnp.float32,
        ).astype(jnp.bfloat16)
        packed = packed.reshape(experts, tensor_size * capacity, model_width)
        arrived = lax.all_to_all(packed, "expert", split_axis=0, concat_axis=0, tiled=True)
        return arrived.reshape(-1, model_width)

    partial_sum = expert_partial(
        send(group_tokens), send(group_grads), gate_weight[0], up_weight[0], down_weight[0]
    )
    summed = lax.psum_scatter(
        partial_sum.reshape(experts, tensor_size * capacity, model_width),
        "tensor",
        scatter_dimension=1,
        tiled=True,
    )
    returned = lax.all_to_all(summed, "expert", split_axis=0, concat_axis=0, tiled=True)
    own_select = lax.dynamic_index_in_dim(select, tensor_index, 0, keepdims=False)
    own = dot(own_select, returned.reshape(experts * capacity, model_width), ((0,), (0,)))
    return lax.all_to_all(
        own.astype(jnp.bfloat16), "tensor", split_axis=1, concat_axis=0, tiled=True
    )


def per_device(tokens, out_grads, species, expert_table, *weights):
    whole = lax.axis_size("tensor") == 1
    experts = expert_table.shape[0]
    by_steps = experts % 4 == 0 and experts & (experts - 1) == 0
    whole = whole and by_steps and (2 * tokens.shape[0] // experts) % 16 == 0
    form = in_halves if whole else in_groups
    return form(tokens, out_grads, species, expert_table, *weights)


def solution(mesh):
    placed = (
        P("expert", "tensor"),
        P("expert", "tensor"),
        P("expert", None),
        P(),
        P("expert", None, "tensor"),
        P("expert", None, "tensor"),
        P("expert", "tensor", None),
    )
    return jax.shard_map(
        per_device, mesh=mesh, in_specs=placed, out_specs=P("expert", "tensor"), check_vma=False
    )
```

```python
import functools

import jax
import jax.numpy as jnp
from jax import lax
from jax.experimental import pallas as pl
from jax.experimental.pallas import tpu as pltpu
from jax.sharding import PartitionSpec as P

PIECES = 2
MIB = 1 << 20


def dot(a, b, contract):
    return lax.dot_general(a, b, (contract, ((), ())), preferred_element_type=jnp.float32)


def hidden_grads(gate_pre, up_pre, hidden_grad):
    sigmoid_gate = jax.nn.sigmoid(gate_pre)
    up_grad = (hidden_grad * gate_pre * sigmoid_gate).astype(jnp.bfloat16)
    gate_grad = (
        hidden_grad * up_pre * sigmoid_gate * (1.0 + gate_pre * (1.0 - sigmoid_gate))
    ).astype(jnp.bfloat16)
    return gate_grad, up_grad


def expert_partial(rows, grads, gate, up, down):
    gate_pre, up_pre = dot(rows, gate, ((1,), (0,))), dot(rows, up, ((1,), (0,)))
    hidden_grad = dot(grads, down, ((1,), (1,)))
    gate_grad, up_grad = hidden_grads(gate_pre, up_pre, hidden_grad)
    partial_sum = dot(gate_grad, gate, ((1,), (1,))) + dot(up_grad, up, ((1,), (1,)))
    return partial_sum.astype(jnp.bfloat16)


def expert_kernel(pair_ref, gate_ref, up_ref, down_ref, out_ref, grads_t, total_t):
    width = out_ref.shape[1]
    step = pl.program_id(0)

    @pl.when(step == 0)
    def _():
        grads_t[...] = pair_ref[:, width:].T
        total_t[...] = jnp.zeros_like(total_t)

    gate, up = gate_ref[0], up_ref[0]
    rows = pair_ref[:, :width]
    gate_pre = dot(rows, gate, ((1,), (0,))).T
    up_pre = dot(rows, up, ((1,), (0,))).T
    hidden_grad = dot(down_ref[0], grads_t[...], ((1,), (0,)))
    gate_grad, up_grad = hidden_grads(gate_pre, up_pre, hidden_grad)
    total_t[...] += dot(gate, gate_grad, ((1,), (0,))) + dot(up, up_grad, ((1,), (0,)))

    @pl.when(step == pl.num_programs(0) - 1)
    def _():
        out_ref[...] = total_t[...].T.astype(out_ref.dtype)


def expert_piece(pair, gate_weight, up_weight, down_weight):
    rows, width = pair.shape[0], pair.shape[1] // 2
    hidden = gate_weight.shape[2]
    tile = min(512, hidden)
    return pl.pallas_call(
        expert_kernel,
        grid=(hidden // tile,),
        in_specs=[
            pl.BlockSpec((rows, 2 * width), lambda i: (0, 0)),
            pl.BlockSpec((1, width, tile), lambda i: (0, 0, i)),
            pl.BlockSpec((1, width, tile), lambda i: (0, 0, i)),
            pl.BlockSpec((1, tile, width), lambda i: (0, i, 0)),
        ],
        out_specs=pl.BlockSpec((rows, width), lambda i: (0, 0)),
        out_shape=jax.ShapeDtypeStruct((rows, width), jnp.bfloat16),
        scratch_shapes=[
            pltpu.VMEM((width, rows), jnp.bfloat16),
            pltpu.VMEM((width, rows), jnp.float32),
        ],
        compiler_params=pltpu.CompilerParams(vmem_limit_bytes=40 * MIB),
        cost_estimate=pl.CostEstimate(
            flops=10 * rows * width * hidden,
            bytes_accessed=6 * width * hidden + 6 * rows * width,
            transcendentals=rows * hidden,
        ),
        name="expert_piece",
    )(pair, gate_weight, up_weight, down_weight)


def place_rows(species, table, depth, pieces):
    experts, rows = table.shape[1], species.shape[1]
    ids = lax.broadcasted_iota(jnp.int32, (experts, rows), 0)
    named = (ids == species).astype(jnp.bfloat16)
    expert_ids = lax.broadcasted_iota(jnp.int32, (experts, experts), 0)
    moved = (expert_ids == table).astype(jnp.bfloat16)
    hits = dot(moved, named, ((1,), (0,)))
    row_ids = lax.broadcasted_iota(jnp.int32, (rows, rows), 0)
    column_ids = lax.broadcasted_iota(jnp.int32, (rows, rows), 1)
    before = (row_ids < column_ids).astype(jnp.bfloat16)
    earlier = dot(hits.astype(jnp.bfloat16), before, ((1,), (0,)))
    slot = jnp.sum(earlier * hits, axis=0, keepdims=True).astype(jnp.int32)
    expert = jnp.sum(ids.astype(jnp.float32) * hits, axis=0, keepdims=True).astype(jnp.int32)
    found = []
    for piece in range(pieces):
        own = slot - piece * depth
        found.append(jnp.where((own >= 0) & (own < depth), expert * depth + own, -1))
    return found


def select_rows(place, count):
    ids = lax.broadcasted_iota(jnp.int32, (count, place.shape[1]), 0)
    return (ids == place).astype(jnp.bfloat16)


def first_kernel(
    depth, species_ref, table_ref, rows_ref, grads_ref, place_ref, out_ref, held, packed, sems
):
    width, part = rows_ref.shape[1], held.shape[2]
    parts = width // part
    sources = [ref.at[:, c * part : (c + 1) * part] for ref in (rows_ref, grads_ref) for c in range(parts)]
    arriving = [
        pltpu.make_async_copy(source, held.at[i], sems.at[0, i]) for i, source in enumerate(sources)
    ]
    leaving = [
        pltpu.make_async_copy(packed.at[i], out_ref.at[:, i * part : (i + 1) * part], sems.at[1, i])
        for i in range(2 * parts)
    ]
    for copy in arriving:
        copy.start()
    place = place_rows(species_ref[...], table_ref[...], depth, place_ref.shape[0])
    for piece, found in enumerate(place):
        place_ref[piece : piece + 1, :] = found
    select = select_rows(place[0], packed.shape[1])
    for i in range(2 * parts):
        arriving[i].wait()
        packed[i] = dot(select, held[i], ((1,), (0,))).astype(packed.dtype)
        leaving[i].start()
    for copy in leaving:
        copy.wait()


def pack_first(species, expert_table, tokens, out_grads, depth, pieces):
    (rows, width), experts = tokens.shape, expert_table.shape[0]
    count, part = experts * depth, min(512, width)
    copies = 2 * width // part
    return pl.pallas_call(
        functools.partial(first_kernel, depth),
        in_specs=[pl.BlockSpec(memory_space=pltpu.VMEM)] * 2 + [pl.BlockSpec(memory_space=pl.ANY)] * 2,
        out_specs=[pl.BlockSpec(memory_space=pltpu.VMEM), pl.BlockSpec(memory_space=pl.ANY)],
        out_shape=[
            jax.ShapeDtypeStruct((pieces, rows), jnp.int32),
            jax.ShapeDtypeStruct((count, 2 * width), jnp.bfloat16),
        ],
        scratch_shapes=[
            pltpu.VMEM((copies, rows, part), jnp.bfloat16),
            pltpu.VMEM((copies, count, part), jnp.bfloat16),
            pltpu.SemaphoreType.DMA((2, copies)),
        ],
        compiler_params=pltpu.CompilerParams(vmem_limit_bytes=60 * MIB),
        name="pack_first",
    )(species.reshape(1, rows), expert_table.reshape(1, experts), tokens, out_grads)


def pack_kernel(piece, place_ref, rows_ref, grads_ref, out_ref):
    count, width = out_ref.shape[0], rows_ref.shape[1]
    select = select_rows(place_ref[piece : piece + 1, :], count)
    out_ref[:, :width] = dot(select, rows_ref[...], ((1,), (0,))).astype(out_ref.dtype)
    out_ref[:, width:] = dot(select, grads_ref[...], ((1,), (0,))).astype(out_ref.dtype)


def pack_pair(place, piece, tokens, out_grads, count):
    rows, width = tokens.shape
    return pl.pallas_call(
        functools.partial(pack_kernel, piece),
        out_shape=jax.ShapeDtypeStruct((count, 2 * width), jnp.bfloat16),
        compiler_params=pltpu.CompilerParams(vmem_limit_bytes=24 * MIB),
        cost_estimate=pl.CostEstimate(
            flops=4 * count * rows * width, bytes_accessed=4 * (rows + count) * width, transcendentals=0
        ),
        name="pack_pair",
    )(place, tokens, out_grads)


def places(species, expert_table, tensor_size):
    experts = expert_table.shape[0]
    rows_dev = species.shape[0] // tensor_size
    expert_ids = jnp.arange(experts, dtype=jnp.int32)
    species_hits = species == expert_ids[None, :]
    expert_of = jnp.sum(jnp.where(species_hits, expert_table[None, :], 0), axis=1).reshape(
        tensor_size, rows_dev
    )
    onehot = (expert_of[:, :, None] == expert_ids[None, None, :]).astype(jnp.int32)
    earlier = jnp.cumsum(onehot, axis=1) - onehot
    slot_of = jnp.sum(earlier * onehot, axis=2)
    return expert_of, slot_of


def in_pieces(tokens, out_grads, species, expert_table, gate_weight, up_weight, down_weight):
    rows_dev, width = tokens.shape
    experts = expert_table.shape[0]
    depth = 2 * rows_dev // experts // PIECES
    count = experts * depth
    place_of, packed = pack_first(species, expert_table, tokens, out_grads, depth, PIECES)
    exchange = functools.partial(
        lax.all_to_all, axis_name="expert", split_axis=0, concat_axis=0, tiled=True
    )
    arrived = [exchange(packed.reshape(experts, depth, 2 * width))]
    for piece in range(1, PIECES):
        packed = pack_pair(place_of, piece, tokens, out_grads, count)
        arrived.append(exchange(packed.reshape(experts, depth, 2 * width)))
    own = None
    for piece in range(PIECES):
        pair = arrived[piece].reshape(count, 2 * width)
        partial_sum = expert_piece(pair, gate_weight, up_weight, down_weight)
        returned = exchange(partial_sum.reshape(experts, depth, width)).reshape(count, width)
        ids = jnp.arange(count, dtype=jnp.int32)
        select = (ids[:, None] == place_of[piece][None, :]).astype(jnp.bfloat16)
        term = dot(select, returned, ((0,), (0,)))
        own = term if own is None else own + term
    return own.astype(jnp.bfloat16)


def in_groups(tokens, out_grads, species, expert_table, gate_weight, up_weight, down_weight):
    tensor_size = lax.axis_size("tensor")
    tensor_index = lax.axis_index("tensor")
    experts = expert_table.shape[0]
    rows_dev = tokens.shape[0] // tensor_size
    model_width = tokens.shape[1] * tensor_size
    capacity = 2 * rows_dev // experts
    expert_of, slot_of = places(species, expert_table, tensor_size)
    group_tokens, group_grads = (
        lax.all_gather(tokens, "tensor", axis=1, tiled=True),
        lax.all_gather(out_grads, "tensor", axis=1, tiled=True),
    )
    place_of = expert_of * capacity + slot_of
    place_ids = jnp.arange(experts * capacity, dtype=jnp.int32)
    select = (place_ids[None, :, None] == place_of[:, None, :]).astype(jnp.bfloat16)

    def send(rows):
        packed = jnp.einsum(
            "tecr,trd->etcd",
            select.reshape(tensor_size, experts, capacity, rows_dev),
            rows.reshape(tensor_size, rows_dev, model_width),
            preferred_element_type=jnp.float32,
        ).astype(jnp.bfloat16)
        packed = packed.reshape(experts, tensor_size * capacity, model_width)
        arrived = lax.all_to_all(packed, "expert", split_axis=0, concat_axis=0, tiled=True)
        return arrived.reshape(-1, model_width)

    partial_sum = expert_partial(
        send(group_tokens), send(group_grads), gate_weight[0], up_weight[0], down_weight[0]
    )
    summed = lax.psum_scatter(
        partial_sum.reshape(experts, tensor_size * capacity, model_width),
        "tensor",
        scatter_dimension=1,
        tiled=True,
    )
    returned = lax.all_to_all(summed, "expert", split_axis=0, concat_axis=0, tiled=True)
    own_select = lax.dynamic_index_in_dim(select, tensor_index, 0, keepdims=False)
    own = dot(own_select, returned.reshape(experts * capacity, model_width), ((0,), (0,)))
    return lax.all_to_all(
        own.astype(jnp.bfloat16), "tensor", split_axis=1, concat_axis=0, tiled=True
    )


def per_device(tokens, out_grads, species, expert_table, *weights):
    whole = lax.axis_size("tensor") == 1
    capacity = 2 * tokens.shape[0] // expert_table.shape[0]
    form = in_pieces if whole and capacity % (8 * PIECES) == 0 else in_groups
    return form(tokens, out_grads, species, expert_table, *weights)


def solution(mesh):
    placed = (
        P("expert", "tensor"),
        P("expert", "tensor"),
        P("expert", None),
        P(),
        P("expert", None, "tensor"),
        P("expert", None, "tensor"),
        P("expert", "tensor", None),
    )
    return jax.shard_map(
        per_device, mesh=mesh, in_specs=placed, out_specs=P("expert", "tensor"), check_vma=False
    )
```

```python
import functools

import jax
import jax.numpy as jnp
from jax import lax
from jax.experimental import pallas as pl
from jax.experimental.pallas import tpu as pltpu
from jax.sharding import PartitionSpec as P

PIECES = 2
MIB = 1 << 20


def dot(a, b, contract):
    return lax.dot_general(a, b, (contract, ((), ())), preferred_element_type=jnp.float32)


def hidden_grads(gate_pre, up_pre, hidden_grad):
    sigmoid_gate = jax.nn.sigmoid(gate_pre)
    up_grad = (hidden_grad * gate_pre * sigmoid_gate).astype(jnp.bfloat16)
    gate_grad = (
        hidden_grad * up_pre * sigmoid_gate * (1.0 + gate_pre * (1.0 - sigmoid_gate))
    ).astype(jnp.bfloat16)
    return gate_grad, up_grad


def expert_partial(rows, grads, gate, up, down):
    gate_pre, up_pre = dot(rows, gate, ((1,), (0,))), dot(rows, up, ((1,), (0,)))
    hidden_grad = dot(grads, down, ((1,), (1,)))
    gate_grad, up_grad = hidden_grads(gate_pre, up_pre, hidden_grad)
    partial_sum = dot(gate_grad, gate, ((1,), (1,))) + dot(up_grad, up, ((1,), (1,)))
    return partial_sum.astype(jnp.bfloat16)


def expert_kernel(
    pair_ref, gate_ref, up_ref, down_ref, out_ref, wide, tall, both, total, sems
):
    width, tile = out_ref.shape[1], tall.shape[1]
    steps = gate_ref.shape[2] // tile
    half, strip = min(256, tile), min(512, width)

    def copies(step, slot):
        part = pl.ds(pl.multiple_of(step * tile, tile), tile)
        return [
            pltpu.make_async_copy(source, target, sems.at[slot, i])
            for i, (source, target) in enumerate(
                (
                    (gate_ref.at[0, :, part], wide.at[slot, :, :tile]),
                    (up_ref.at[0, :, part], wide.at[slot, :, tile:]),
                    (down_ref.at[0, part, :], tall.at[slot]),
                )
            )
        ]

    for copy in copies(0, 0):
        copy.start()
    total[...] = jnp.zeros_like(total)

    def body(step, carry):
        slot = lax.rem(step, 2)

        @pl.when(step + 1 < steps)
        def _():
            for copy in copies(step + 1, 1 - slot):
                copy.start()

        for copy in copies(step, slot):
            copy.wait()
        rows, grads = pair_ref[:, :width], pair_ref[:, width:]
        for low in range(0, tile, half):
            high = low + half
            gate_pre = dot(rows, wide[slot, :, low:high], ((1,), (0,)))
            up_pre = dot(rows, wide[slot, :, tile + low : tile + high], ((1,), (0,)))
            hidden_grad = dot(grads, tall[slot, low:high, :], ((1,), (1,)))
            gate_grad, up_grad = hidden_grads(gate_pre, up_pre, hidden_grad)
            both[:, low:high] = gate_grad
            both[:, tile + low : tile + high] = up_grad
        for low in range(0, width, strip):
            high = low + strip
            total[:, low:high] += dot(both[...], wide[slot, low:high, :], ((1,), (1,)))
        return carry

    lax.fori_loop(0, steps, body, 0)
    out_ref[...] = total[...].astype(out_ref.dtype)


def expert_piece(pair, gate_weight, up_weight, down_weight):
    rows, width = pair.shape[0], pair.shape[1] // 2
    hidden = gate_weight.shape[2]
    tile = min(512, hidden)
    return pl.pallas_call(
        expert_kernel,
        in_specs=[pl.BlockSpec(memory_space=pltpu.VMEM)] + [pl.BlockSpec(memory_space=pl.ANY)] * 3,
        out_specs=pl.BlockSpec(memory_space=pltpu.VMEM),
        out_shape=jax.ShapeDtypeStruct((rows, width), jnp.bfloat16),
        scratch_shapes=[
            pltpu.VMEM((2, width, 2 * tile), jnp.bfloat16),
            pltpu.VMEM((2, tile, width), jnp.bfloat16),
            pltpu.VMEM((rows, 2 * tile), jnp.bfloat16),
            pltpu.VMEM((rows, width), jnp.float32),
            pltpu.SemaphoreType.DMA((2, 3)),
        ],
        compiler_params=pltpu.CompilerParams(vmem_limit_bytes=40 * MIB),
        cost_estimate=pl.CostEstimate(
            flops=10 * rows * width * hidden,
            bytes_accessed=6 * width * hidden + 6 * rows * width,
            transcendentals=rows * hidden,
        ),
        name="expert_piece",
    )(pair, gate_weight, up_weight, down_weight)


def place_rows(species, table, depth, pieces):
    experts, rows = table.shape[1], species.shape[1]
    ids = lax.broadcasted_iota(jnp.int32, (experts, rows), 0)
    named = (ids == species).astype(jnp.bfloat16)
    expert_ids = lax.broadcasted_iota(jnp.int32, (experts, experts), 0)
    moved = (expert_ids == table).astype(jnp.bfloat16)
    hits = dot(moved, named, ((1,), (0,)))
    row_ids = lax.broadcasted_iota(jnp.int32, (rows, rows), 0)
    column_ids = lax.broadcasted_iota(jnp.int32, (rows, rows), 1)
    before = (row_ids < column_ids).astype(jnp.bfloat16)
    earlier = dot(hits.astype(jnp.bfloat16), before, ((1,), (0,)))
    slot = jnp.sum(earlier * hits, axis=0, keepdims=True).astype(jnp.int32)
    expert = jnp.sum(ids.astype(jnp.float32) * hits, axis=0, keepdims=True).astype(jnp.int32)
    found = []
    for piece in range(pieces):
        own = slot - piece * depth
        found.append(jnp.where((own >= 0) & (own < depth), expert * depth + own, -1))
    return found


def select_rows(place, count):
    ids = lax.broadcasted_iota(jnp.int32, (count, place.shape[1]), 0)
    return (ids == place).astype(jnp.bfloat16)


def first_kernel(
    depth, species_ref, table_ref, rows_ref, grads_ref, place_ref, out_ref, held, packed, sems
):
    width, part = rows_ref.shape[1], held.shape[2]
    parts = width // part
    sources = [ref.at[:, c * part : (c + 1) * part] for ref in (rows_ref, grads_ref) for c in range(parts)]
    arriving = [
        pltpu.make_async_copy(source, held.at[i], sems.at[0, i]) for i, source in enumerate(sources)
    ]
    leaving = [
        pltpu.make_async_copy(packed.at[i], out_ref.at[:, i * part : (i + 1) * part], sems.at[1, i])
        for i in range(2 * parts)
    ]
    for copy in arriving:
        copy.start()
    place = place_rows(species_ref[...], table_ref[...], depth, place_ref.shape[0])
    for piece, found in enumerate(place):
        place_ref[piece : piece + 1, :] = found
    select = select_rows(place[0], packed.shape[1])
    for i in range(2 * parts):
        arriving[i].wait()
        packed[i] = dot(select, held[i], ((1,), (0,))).astype(packed.dtype)
        leaving[i].start()
    for copy in leaving:
        copy.wait()


def pack_first(species, expert_table, tokens, out_grads, depth, pieces):
    (rows, width), experts = tokens.shape, expert_table.shape[0]
    count, part = experts * depth, min(512, width)
    copies = 2 * width // part
    return pl.pallas_call(
        functools.partial(first_kernel, depth),
        in_specs=[pl.BlockSpec(memory_space=pltpu.VMEM)] * 2 + [pl.BlockSpec(memory_space=pl.ANY)] * 2,
        out_specs=[pl.BlockSpec(memory_space=pltpu.VMEM), pl.BlockSpec(memory_space=pl.ANY)],
        out_shape=[
            jax.ShapeDtypeStruct((pieces, rows), jnp.int32),
            jax.ShapeDtypeStruct((count, 2 * width), jnp.bfloat16),
        ],
        scratch_shapes=[
            pltpu.VMEM((copies, rows, part), jnp.bfloat16),
            pltpu.VMEM((copies, count, part), jnp.bfloat16),
            pltpu.SemaphoreType.DMA((2, copies)),
        ],
        compiler_params=pltpu.CompilerParams(vmem_limit_bytes=60 * MIB),
        name="pack_first",
    )(species.reshape(1, rows), expert_table.reshape(1, experts), tokens, out_grads)


def pack_kernel(piece, place_ref, rows_ref, grads_ref, out_ref):
    count, width = out_ref.shape[0], rows_ref.shape[1]
    select = select_rows(place_ref[piece : piece + 1, :], count)
    out_ref[:, :width] = dot(select, rows_ref[...], ((1,), (0,))).astype(out_ref.dtype)
    out_ref[:, width:] = dot(select, grads_ref[...], ((1,), (0,))).astype(out_ref.dtype)


def pack_pair(place, piece, tokens, out_grads, count):
    rows, width = tokens.shape
    return pl.pallas_call(
        functools.partial(pack_kernel, piece),
        out_shape=jax.ShapeDtypeStruct((count, 2 * width), jnp.bfloat16),
        compiler_params=pltpu.CompilerParams(vmem_limit_bytes=24 * MIB),
        cost_estimate=pl.CostEstimate(
            flops=4 * count * rows * width, bytes_accessed=4 * (rows + count) * width, transcendentals=0
        ),
        name="pack_pair",
    )(place, tokens, out_grads)


def places(species, expert_table, tensor_size):
    experts = expert_table.shape[0]
    rows_dev = species.shape[0] // tensor_size
    expert_ids = jnp.arange(experts, dtype=jnp.int32)
    species_hits = species == expert_ids[None, :]
    expert_of = jnp.sum(jnp.where(species_hits, expert_table[None, :], 0), axis=1).reshape(
        tensor_size, rows_dev
    )
    onehot = (expert_of[:, :, None] == expert_ids[None, None, :]).astype(jnp.int32)
    earlier = jnp.cumsum(onehot, axis=1) - onehot
    slot_of = jnp.sum(earlier * onehot, axis=2)
    return expert_of, slot_of


def in_pieces(tokens, out_grads, species, expert_table, gate_weight, up_weight, down_weight):
    rows_dev, width = tokens.shape
    experts = expert_table.shape[0]
    depth = 2 * rows_dev // experts // PIECES
    count = experts * depth
    place_of, packed = pack_first(species, expert_table, tokens, out_grads, depth, PIECES)
    exchange = functools.partial(
        lax.all_to_all, axis_name="expert", split_axis=0, concat_axis=0, tiled=True
    )
    arrived = [exchange(packed.reshape(experts, depth, 2 * width))]
    for piece in range(1, PIECES):
        packed = pack_pair(place_of, piece, tokens, out_grads, count)
        arrived.append(exchange(packed.reshape(experts, depth, 2 * width)))
    own = None
    for piece in range(PIECES):
        pair = arrived[piece].reshape(count, 2 * width)
        partial_sum = expert_piece(pair, gate_weight, up_weight, down_weight)
        returned = exchange(partial_sum.reshape(experts, depth, width)).reshape(count, width)
        ids = jnp.arange(count, dtype=jnp.int32)
        select = (ids[:, None] == place_of[piece][None, :]).astype(jnp.bfloat16)
        term = dot(select, returned, ((0,), (0,)))
        own = term if own is None else own + term
    return own.astype(jnp.bfloat16)


def in_groups(tokens, out_grads, species, expert_table, gate_weight, up_weight, down_weight):
    tensor_size = lax.axis_size("tensor")
    tensor_index = lax.axis_index("tensor")
    experts = expert_table.shape[0]
    rows_dev = tokens.shape[0] // tensor_size
    model_width = tokens.shape[1] * tensor_size
    capacity = 2 * rows_dev // experts
    expert_of, slot_of = places(species, expert_table, tensor_size)
    group_tokens, group_grads = (
        lax.all_gather(tokens, "tensor", axis=1, tiled=True),
        lax.all_gather(out_grads, "tensor", axis=1, tiled=True),
    )
    place_of = expert_of * capacity + slot_of
    place_ids = jnp.arange(experts * capacity, dtype=jnp.int32)
    select = (place_ids[None, :, None] == place_of[:, None, :]).astype(jnp.bfloat16)

    def send(rows):
        packed = jnp.einsum(
            "tecr,trd->etcd",
            select.reshape(tensor_size, experts, capacity, rows_dev),
            rows.reshape(tensor_size, rows_dev, model_width),
            preferred_element_type=jnp.float32,
        ).astype(jnp.bfloat16)
        packed = packed.reshape(experts, tensor_size * capacity, model_width)
        arrived = lax.all_to_all(packed, "expert", split_axis=0, concat_axis=0, tiled=True)
        return arrived.reshape(-1, model_width)

    partial_sum = expert_partial(
        send(group_tokens), send(group_grads), gate_weight[0], up_weight[0], down_weight[0]
    )
    summed = lax.psum_scatter(
        partial_sum.reshape(experts, tensor_size * capacity, model_width),
        "tensor",
        scatter_dimension=1,
        tiled=True,
    )
    returned = lax.all_to_all(summed, "expert", split_axis=0, concat_axis=0, tiled=True)
    own_select = lax.dynamic_index_in_dim(select, tensor_index, 0, keepdims=False)
    own = dot(own_select, returned.reshape(experts * capacity, model_width), ((0,), (0,)))
    return lax.all_to_all(
        own.astype(jnp.bfloat16), "tensor", split_axis=1, concat_axis=0, tiled=True
    )


def per_device(tokens, out_grads, species, expert_table, *weights):
    whole = lax.axis_size("tensor") == 1
    capacity = 2 * tokens.shape[0] // expert_table.shape[0]
    form = in_pieces if whole and capacity % (8 * PIECES) == 0 else in_groups
    return form(tokens, out_grads, species, expert_table, *weights)


def solution(mesh):
    placed = (
        P("expert", "tensor"),
        P("expert", "tensor"),
        P("expert", None),
        P(),
        P("expert", None, "tensor"),
        P("expert", None, "tensor"),
        P("expert", "tensor", None),
    )
    return jax.shard_map(
        per_device, mesh=mesh, in_specs=placed, out_specs=P("expert", "tensor"), check_vma=False
    )
```

```python
import functools

import jax
import jax.numpy as jnp
from jax import lax
from jax.experimental import pallas as pl
from jax.experimental.pallas import tpu as pltpu
from jax.sharding import PartitionSpec as P

PIECES = 2
MIB = 1 << 20


def dot(a, b, contract):
    return lax.dot_general(a, b, (contract, ((), ())), preferred_element_type=jnp.float32)


def hidden_grads(gate_pre, up_pre, hidden_grad):
    sigmoid_gate = jax.nn.sigmoid(gate_pre)
    up_grad = (hidden_grad * gate_pre * sigmoid_gate).astype(jnp.bfloat16)
    gate_grad = (
        hidden_grad * up_pre * sigmoid_gate * (1.0 + gate_pre * (1.0 - sigmoid_gate))
    ).astype(jnp.bfloat16)
    return gate_grad, up_grad


def expert_partial(rows, grads, gate, up, down):
    gate_pre, up_pre = dot(rows, gate, ((1,), (0,))), dot(rows, up, ((1,), (0,)))
    hidden_grad = dot(grads, down, ((1,), (1,)))
    gate_grad, up_grad = hidden_grads(gate_pre, up_pre, hidden_grad)
    partial_sum = dot(gate_grad, gate, ((1,), (1,))) + dot(up_grad, up, ((1,), (1,)))
    return partial_sum.astype(jnp.bfloat16)


def parts_of(source, target, parts):
    rows = source.shape[0] // parts
    for i in range(parts):
        part = slice(i * rows, (i + 1) * rows)
        yield source.at[part], target.at[part]


def expert_kernel(
    pair_ref, gate_ref, up_ref, down_ref, out_ref, pair, wide, tall, both, total, leaving, pair_sems, sems, out_sems
):
    width, tile = out_ref.shape[1], tall.shape[1]
    steps = gate_ref.shape[2] // tile
    half, strip = min(256, tile), leaving.shape[2]
    slots, cuts = wide.shape[0], sems.shape[2]

    def copies(step, slot):
        part = pl.ds(pl.multiple_of(step * tile, tile), tile)
        pairs = (
            (gate_ref.at[0, :, part], wide.at[slot, :, :tile]),
            (up_ref.at[0, :, part], wide.at[slot, :, tile:]),
            (down_ref.at[0, part, :], tall.at[slot]),
        )
        return [
            pltpu.make_async_copy(source, target, sems.at[slot, i, k])
            for i, (whole, held) in enumerate(pairs)
            for k, (source, target) in enumerate(parts_of(whole, held, cuts))
        ]

    arriving = [
        pltpu.make_async_copy(source, target, pair_sems.at[k])
        for k, (source, target) in enumerate(parts_of(pair_ref, pair, pair_sems.shape[0]))
    ]
    for copy in arriving + copies(0, 0):
        copy.start()
    for step in range(1, min(slots - 1, steps)):
        for copy in copies(step, step):
            copy.start()
    total[...] = jnp.zeros_like(total)
    for copy in arriving:
        copy.wait()

    def body(step, carry):
        slot = lax.rem(step, slots)
        ahead = step + slots - 1

        @pl.when(ahead < steps)
        def _():
            for copy in copies(ahead, lax.rem(ahead, slots)):
                copy.start()

        for copy in copies(step, slot):
            copy.wait()
        rows, grads = pair[:, :width], pair[:, width:]
        for low in range(0, tile, half):
            high = low + half
            gate_pre = dot(rows, wide[slot, :, low:high], ((1,), (0,)))
            up_pre = dot(rows, wide[slot, :, tile + low : tile + high], ((1,), (0,)))
            hidden_grad = dot(grads, tall[slot, low:high, :], ((1,), (1,)))
            gate_grad, up_grad = hidden_grads(gate_pre, up_pre, hidden_grad)
            both[:, low:high] = gate_grad
            both[:, tile + low : tile + high] = up_grad
        for low in range(0, width, strip):
            high = low + strip
            total[:, low:high] += dot(both[...], wide[slot, low:high, :], ((1,), (1,)))
        return carry

    lax.fori_loop(0, steps, body, 0)
    results = []
    for i in range(width // strip):
        columns = slice(i * strip, (i + 1) * strip)
        leaving[i] = total[:, columns].astype(leaving.dtype)
        results.append(pltpu.make_async_copy(leaving.at[i], out_ref.at[:, columns], out_sems.at[i]))
        results[-1].start()
    for copy in results:
        copy.wait()


def expert_piece(pair, gate_weight, up_weight, down_weight):
    rows, width = pair.shape[0], pair.shape[1] // 2
    hidden = gate_weight.shape[2]
    tile, strip = min(512, hidden), min(512, width)
    slots, cuts = 3, 4
    return pl.pallas_call(
        expert_kernel,
        in_specs=[pl.BlockSpec(memory_space=pl.ANY)] * 4,
        out_specs=pl.BlockSpec(memory_space=pl.ANY),
        out_shape=jax.ShapeDtypeStruct((rows, width), jnp.bfloat16),
        scratch_shapes=[
            pltpu.VMEM((rows, 2 * width), jnp.bfloat16),
            pltpu.VMEM((slots, width, 2 * tile), jnp.bfloat16),
            pltpu.VMEM((slots, tile, width), jnp.bfloat16),
            pltpu.VMEM((rows, 2 * tile), jnp.bfloat16),
            pltpu.VMEM((rows, width), jnp.float32),
            pltpu.VMEM((width // strip, rows, strip), jnp.bfloat16),
            pltpu.SemaphoreType.DMA((4,)),
            pltpu.SemaphoreType.DMA((slots, 3, cuts)),
            pltpu.SemaphoreType.DMA((width // strip,)),
        ],
        compiler_params=pltpu.CompilerParams(vmem_limit_bytes=56 * MIB),
        cost_estimate=pl.CostEstimate(
            flops=10 * rows * width * hidden,
            bytes_accessed=6 * width * hidden + 6 * rows * width,
            transcendentals=rows * hidden,
        ),
        name="expert_piece",
    )(pair, gate_weight, up_weight, down_weight)


def place_rows(species, table, depth, pieces):
    experts, rows = table.shape[1], species.shape[1]
    ids = lax.broadcasted_iota(jnp.int32, (experts, rows), 0)
    named = (ids == species).astype(jnp.bfloat16)
    expert_ids = lax.broadcasted_iota(jnp.int32, (experts, experts), 0)
    moved = (expert_ids == table).astype(jnp.bfloat16)
    hits = dot(moved, named, ((1,), (0,)))
    row_ids = lax.broadcasted_iota(jnp.int32, (rows, rows), 0)
    column_ids = lax.broadcasted_iota(jnp.int32, (rows, rows), 1)
    before = (row_ids < column_ids).astype(jnp.bfloat16)
    earlier = dot(hits.astype(jnp.bfloat16), before, ((1,), (0,)))
    slot = jnp.sum(earlier * hits, axis=0, keepdims=True).astype(jnp.int32)
    expert = jnp.sum(ids.astype(jnp.float32) * hits, axis=0, keepdims=True).astype(jnp.int32)
    found = []
    for piece in range(pieces):
        own = slot - piece * depth
        found.append(jnp.where((own >= 0) & (own < depth), expert * depth + own, -1))
    return found


def select_rows(place, count):
    ids = lax.broadcasted_iota(jnp.int32, (count, place.shape[1]), 0)
    return (ids == place).astype(jnp.bfloat16)


def first_kernel(
    depth, species_ref, table_ref, rows_ref, grads_ref, place_ref, out_ref, held, packed, sems
):
    width, part = rows_ref.shape[1], held.shape[2]
    parts = width // part
    sources = [ref.at[:, c * part : (c + 1) * part] for ref in (rows_ref, grads_ref) for c in range(parts)]
    arriving = [
        pltpu.make_async_copy(source, held.at[i], sems.at[0, i]) for i, source in enumerate(sources)
    ]
    leaving = [
        pltpu.make_async_copy(packed.at[i], out_ref.at[:, i * part : (i + 1) * part], sems.at[1, i])
        for i in range(2 * parts)
    ]
    for copy in arriving:
        copy.start()
    place = place_rows(species_ref[...], table_ref[...], depth, place_ref.shape[0])
    for piece, found in enumerate(place):
        place_ref[piece : piece + 1, :] = found
    select = select_rows(place[0], packed.shape[1])
    for i in range(2 * parts):
        arriving[i].wait()
        packed[i] = dot(select, held[i], ((1,), (0,))).astype(packed.dtype)
        leaving[i].start()
    for copy in leaving:
        copy.wait()


def pack_first(species, expert_table, tokens, out_grads, depth, pieces):
    (rows, width), experts = tokens.shape, expert_table.shape[0]
    count, part = experts * depth, min(512, width)
    copies = 2 * width // part
    return pl.pallas_call(
        functools.partial(first_kernel, depth),
        in_specs=[pl.BlockSpec(memory_space=pltpu.VMEM)] * 2 + [pl.BlockSpec(memory_space=pl.ANY)] * 2,
        out_specs=[pl.BlockSpec(memory_space=pltpu.VMEM), pl.BlockSpec(memory_space=pl.ANY)],
        out_shape=[
            jax.ShapeDtypeStruct((pieces, rows), jnp.int32),
            jax.ShapeDtypeStruct((count, 2 * width), jnp.bfloat16),
        ],
        scratch_shapes=[
            pltpu.VMEM((copies, rows, part), jnp.bfloat16),
            pltpu.VMEM((copies, count, part), jnp.bfloat16),
            pltpu.SemaphoreType.DMA((2, copies)),
        ],
        compiler_params=pltpu.CompilerParams(vmem_limit_bytes=60 * MIB),
        name="pack_first",
    )(species.reshape(1, rows), expert_table.reshape(1, experts), tokens, out_grads)


def pack_kernel(piece, place_ref, rows_ref, grads_ref, out_ref):
    count, width = out_ref.shape[0], rows_ref.shape[1]
    select = select_rows(place_ref[piece : piece + 1, :], count)
    out_ref[:, :width] = dot(select, rows_ref[...], ((1,), (0,))).astype(out_ref.dtype)
    out_ref[:, width:] = dot(select, grads_ref[...], ((1,), (0,))).astype(out_ref.dtype)


def pack_pair(place, piece, tokens, out_grads, count):
    rows, width = tokens.shape
    return pl.pallas_call(
        functools.partial(pack_kernel, piece),
        out_shape=jax.ShapeDtypeStruct((count, 2 * width), jnp.bfloat16),
        compiler_params=pltpu.CompilerParams(vmem_limit_bytes=24 * MIB),
        cost_estimate=pl.CostEstimate(
            flops=4 * count * rows * width, bytes_accessed=4 * (rows + count) * width, transcendentals=0
        ),
        name="pack_pair",
    )(place, tokens, out_grads)


def places(species, expert_table, tensor_size):
    experts = expert_table.shape[0]
    rows_dev = species.shape[0] // tensor_size
    expert_ids = jnp.arange(experts, dtype=jnp.int32)
    species_hits = species == expert_ids[None, :]
    expert_of = jnp.sum(jnp.where(species_hits, expert_table[None, :], 0), axis=1).reshape(
        tensor_size, rows_dev
    )
    onehot = (expert_of[:, :, None] == expert_ids[None, None, :]).astype(jnp.int32)
    earlier = jnp.cumsum(onehot, axis=1) - onehot
    slot_of = jnp.sum(earlier * onehot, axis=2)
    return expert_of, slot_of


def in_pieces(tokens, out_grads, species, expert_table, gate_weight, up_weight, down_weight):
    rows_dev, width = tokens.shape
    experts = expert_table.shape[0]
    depth = 2 * rows_dev // experts // PIECES
    count = experts * depth
    place_of, packed = pack_first(species, expert_table, tokens, out_grads, depth, PIECES)
    exchange = functools.partial(
        lax.all_to_all, axis_name="expert", split_axis=0, concat_axis=0, tiled=True
    )
    arrived = [exchange(packed.reshape(experts, depth, 2 * width))]
    for piece in range(1, PIECES):
        packed = pack_pair(place_of, piece, tokens, out_grads, count)
        arrived.append(exchange(packed.reshape(experts, depth, 2 * width)))
    own = None
    for piece in range(PIECES):
        pair = arrived[piece].reshape(count, 2 * width)
        partial_sum = expert_piece(pair, gate_weight, up_weight, down_weight)
        returned = exchange(partial_sum.reshape(experts, depth, width)).reshape(count, width)
        ids = jnp.arange(count, dtype=jnp.int32)
        select = (ids[:, None] == place_of[piece][None, :]).astype(jnp.bfloat16)
        term = dot(select, returned, ((0,), (0,)))
        own = term if own is None else own + term
    return own.astype(jnp.bfloat16)


def in_groups(tokens, out_grads, species, expert_table, gate_weight, up_weight, down_weight):
    tensor_size = lax.axis_size("tensor")
    tensor_index = lax.axis_index("tensor")
    experts = expert_table.shape[0]
    rows_dev = tokens.shape[0] // tensor_size
    model_width = tokens.shape[1] * tensor_size
    capacity = 2 * rows_dev // experts
    expert_of, slot_of = places(species, expert_table, tensor_size)
    group_tokens, group_grads = (
        lax.all_gather(tokens, "tensor", axis=1, tiled=True),
        lax.all_gather(out_grads, "tensor", axis=1, tiled=True),
    )
    place_of = expert_of * capacity + slot_of
    place_ids = jnp.arange(experts * capacity, dtype=jnp.int32)
    select = (place_ids[None, :, None] == place_of[:, None, :]).astype(jnp.bfloat16)

    def send(rows):
        packed = jnp.einsum(
            "tecr,trd->etcd",
            select.reshape(tensor_size, experts, capacity, rows_dev),
            rows.reshape(tensor_size, rows_dev, model_width),
            preferred_element_type=jnp.float32,
        ).astype(jnp.bfloat16)
        packed = packed.reshape(experts, tensor_size * capacity, model_width)
        arrived = lax.all_to_all(packed, "expert", split_axis=0, concat_axis=0, tiled=True)
        return arrived.reshape(-1, model_width)

    partial_sum = expert_partial(
        send(group_tokens), send(group_grads), gate_weight[0], up_weight[0], down_weight[0]
    )
    summed = lax.psum_scatter(
        partial_sum.reshape(experts, tensor_size * capacity, model_width),
        "tensor",
        scatter_dimension=1,
        tiled=True,
    )
    returned = lax.all_to_all(summed, "expert", split_axis=0, concat_axis=0, tiled=True)
    own_select = lax.dynamic_index_in_dim(select, tensor_index, 0, keepdims=False)
    own = dot(own_select, returned.reshape(experts * capacity, model_width), ((0,), (0,)))
    return lax.all_to_all(
        own.astype(jnp.bfloat16), "tensor", split_axis=1, concat_axis=0, tiled=True
    )


def per_device(tokens, out_grads, species, expert_table, *weights):
    whole = lax.axis_size("tensor") == 1
    capacity = 2 * tokens.shape[0] // expert_table.shape[0]
    form = in_pieces if whole and capacity % (8 * PIECES) == 0 else in_groups
    return form(tokens, out_grads, species, expert_table, *weights)


def solution(mesh):
    placed = (
        P("expert", "tensor"),
        P("expert", "tensor"),
        P("expert", None),
        P(),
        P("expert", None, "tensor"),
        P("expert", None, "tensor"),
        P("expert", "tensor", None),
    )
    return jax.shard_map(
        per_device, mesh=mesh, in_specs=placed, out_specs=P("expert", "tensor"), check_vma=False
    )
```

```python
import functools

import jax
import jax.numpy as jnp
from jax import lax
from jax.experimental import pallas as pl
from jax.experimental.pallas import tpu as pltpu
from jax.sharding import PartitionSpec as P

PIECES = 2
MIB = 1 << 20


def dot(a, b, contract):
    return lax.dot_general(a, b, (contract, ((), ())), preferred_element_type=jnp.float32)


def hidden_grads(gate_pre, up_pre, hidden_grad):
    sigmoid_gate = jax.nn.sigmoid(gate_pre)
    up_grad = (hidden_grad * gate_pre * sigmoid_gate).astype(jnp.bfloat16)
    gate_grad = (
        hidden_grad * up_pre * sigmoid_gate * (1.0 + gate_pre * (1.0 - sigmoid_gate))
    ).astype(jnp.bfloat16)
    return gate_grad, up_grad


def expert_partial(rows, grads, gate, up, down):
    gate_pre, up_pre = dot(rows, gate, ((1,), (0,))), dot(rows, up, ((1,), (0,)))
    hidden_grad = dot(grads, down, ((1,), (1,)))
    gate_grad, up_grad = hidden_grads(gate_pre, up_pre, hidden_grad)
    partial_sum = dot(gate_grad, gate, ((1,), (1,))) + dot(up_grad, up, ((1,), (1,)))
    return partial_sum.astype(jnp.bfloat16)


def expert_kernel(
    pair_ref, gate_ref, up_ref, down_ref, out_ref, wide, tall, both, total, sems
):
    width, tile = out_ref.shape[1], tall.shape[1]
    steps = gate_ref.shape[2] // tile
    half, strip = min(256, tile), min(512, width)

    def copies(step, slot):
        part = pl.ds(pl.multiple_of(step * tile, tile), tile)
        return [
            pltpu.make_async_copy(source, target, sems.at[slot, i])
            for i, (source, target) in enumerate(
                (
                    (gate_ref.at[0, :, part], wide.at[slot, :, :tile]),
                    (up_ref.at[0, :, part], wide.at[slot, :, tile:]),
                    (down_ref.at[0, part, :], tall.at[slot]),
                )
            )
        ]

    for copy in copies(0, 0):
        copy.start()
    total[...] = jnp.zeros_like(total)

    def body(step, carry):
        slot = lax.rem(step, 2)

        @pl.when(step + 1 < steps)
        def _():
            for copy in copies(step + 1, 1 - slot):
                copy.start()

        for copy in copies(step, slot):
            copy.wait()
        rows, grads = pair_ref[:, :width], pair_ref[:, width:]
        for low in range(0, tile, half):
            high = low + half
            gate_pre = dot(rows, wide[slot, :, low:high], ((1,), (0,)))
            up_pre = dot(rows, wide[slot, :, tile + low : tile + high], ((1,), (0,)))
            hidden_grad = dot(grads, tall[slot, low:high, :], ((1,), (1,)))
            gate_grad, up_grad = hidden_grads(gate_pre, up_pre, hidden_grad)
            both[:, low:high] = gate_grad
            both[:, tile + low : tile + high] = up_grad
        for low in range(0, width, strip):
            high = low + strip
            total[:, low:high] += dot(both[...], wide[slot, low:high, :], ((1,), (1,)))
        return carry

    lax.fori_loop(0, steps, body, 0)
    out_ref[...] = total[...].astype(out_ref.dtype)


def expert_piece(pair, gate_weight, up_weight, down_weight):
    rows, width = pair.shape[0], pair.shape[1] // 2
    hidden = gate_weight.shape[2]
    tile = min(512, hidden)
    return pl.pallas_call(
        expert_kernel,
        in_specs=[pl.BlockSpec(memory_space=pltpu.VMEM)] + [pl.BlockSpec(memory_space=pl.ANY)] * 3,
        out_specs=pl.BlockSpec(memory_space=pltpu.VMEM),
        out_shape=jax.ShapeDtypeStruct((rows, width), jnp.bfloat16),
        scratch_shapes=[
            pltpu.VMEM((2, width, 2 * tile), jnp.bfloat16),
            pltpu.VMEM((2, tile, width), jnp.bfloat16),
            pltpu.VMEM((rows, 2 * tile), jnp.bfloat16),
            pltpu.VMEM((rows, width), jnp.float32),
            pltpu.SemaphoreType.DMA((2, 3)),
        ],
        compiler_params=pltpu.CompilerParams(vmem_limit_bytes=40 * MIB),
        cost_estimate=pl.CostEstimate(
            flops=10 * rows * width * hidden,
            bytes_accessed=6 * width * hidden + 6 * rows * width,
            transcendentals=rows * hidden,
        ),
        name="expert_piece",
    )(pair, gate_weight, up_weight, down_weight)


def turn_of(device, count):
    quarter = device // (count // 4)
    return device % (count // 4) * 4 + quarter % 2 * 2 + quarter // 2


def place_rows(species, table, depth, pieces):
    experts, rows = table.shape[1], species.shape[1]
    ids = lax.broadcasted_iota(jnp.int32, (experts, rows), 0)
    named = (ids == species).astype(jnp.bfloat16)
    expert_ids = lax.broadcasted_iota(jnp.int32, (experts, experts), 0)
    moved = (expert_ids == table).astype(jnp.bfloat16)
    hits = dot(moved, named, ((1,), (0,)))
    row_ids = lax.broadcasted_iota(jnp.int32, (rows, rows), 0)
    column_ids = lax.broadcasted_iota(jnp.int32, (rows, rows), 1)
    before = (row_ids < column_ids).astype(jnp.bfloat16)
    earlier = dot(hits.astype(jnp.bfloat16), before, ((1,), (0,)))
    slot = jnp.sum(earlier * hits, axis=0, keepdims=True).astype(jnp.int32)
    turn = turn_of(ids, experts).astype(jnp.float32)
    expert = jnp.sum(turn * hits, axis=0, keepdims=True).astype(jnp.int32)
    found = []
    for piece in range(pieces):
        own = slot - piece * depth
        found.append(jnp.where((own >= 0) & (own < depth), expert * depth + own, -1))
    return found


def select_rows(place, count):
    ids = lax.broadcasted_iota(jnp.int32, (count, place.shape[1]), 0)
    return (ids == place).astype(jnp.bfloat16)


def first_kernel(
    depth, species_ref, table_ref, rows_ref, grads_ref, place_ref, out_ref, held, packed, sems
):
    width, part = rows_ref.shape[1], held.shape[2]
    parts = width // part
    sources = [ref.at[:, c * part : (c + 1) * part] for ref in (rows_ref, grads_ref) for c in range(parts)]
    arriving = [
        pltpu.make_async_copy(source, held.at[i], sems.at[0, i]) for i, source in enumerate(sources)
    ]
    leaving = [
        pltpu.make_async_copy(packed.at[i], out_ref.at[:, i * part : (i + 1) * part], sems.at[1, i])
        for i in range(2 * parts)
    ]
    for copy in arriving:
        copy.start()
    place = place_rows(species_ref[...], table_ref[...], depth, place_ref.shape[0])
    for piece, found in enumerate(place):
        place_ref[piece : piece + 1, :] = found
    select = select_rows(place[0], packed.shape[1])
    for i in range(2 * parts):
        arriving[i].wait()
        packed[i] = dot(select, held[i], ((1,), (0,))).astype(packed.dtype)
        leaving[i].start()
    for copy in leaving:
        copy.wait()


def pack_first(species, expert_table, tokens, out_grads, depth, pieces):
    (rows, width), experts = tokens.shape, expert_table.shape[0]
    count, part = experts * depth, min(512, width)
    copies = 2 * width // part
    return pl.pallas_call(
        functools.partial(first_kernel, depth),
        in_specs=[pl.BlockSpec(memory_space=pltpu.VMEM)] * 2 + [pl.BlockSpec(memory_space=pl.ANY)] * 2,
        out_specs=[pl.BlockSpec(memory_space=pltpu.VMEM), pl.BlockSpec(memory_space=pl.ANY)],
        out_shape=[
            jax.ShapeDtypeStruct((pieces, rows), jnp.int32),
            jax.ShapeDtypeStruct((count, 2 * width), jnp.bfloat16),
        ],
        scratch_shapes=[
            pltpu.VMEM((copies, rows, part), jnp.bfloat16),
            pltpu.VMEM((copies, count, part), jnp.bfloat16),
            pltpu.SemaphoreType.DMA((2, copies)),
        ],
        compiler_params=pltpu.CompilerParams(vmem_limit_bytes=60 * MIB),
        name="pack_first",
    )(species.reshape(1, rows), expert_table.reshape(1, experts), tokens, out_grads)


def pack_kernel(piece, place_ref, rows_ref, grads_ref, out_ref):
    count, width = out_ref.shape[0], rows_ref.shape[1]
    select = select_rows(place_ref[piece : piece + 1, :], count)
    out_ref[:, :width] = dot(select, rows_ref[...], ((1,), (0,))).astype(out_ref.dtype)
    out_ref[:, width:] = dot(select, grads_ref[...], ((1,), (0,))).astype(out_ref.dtype)


def pack_pair(place, piece, tokens, out_grads, count):
    rows, width = tokens.shape
    return pl.pallas_call(
        functools.partial(pack_kernel, piece),
        out_shape=jax.ShapeDtypeStruct((count, 2 * width), jnp.bfloat16),
        compiler_params=pltpu.CompilerParams(vmem_limit_bytes=24 * MIB),
        cost_estimate=pl.CostEstimate(
            flops=4 * count * rows * width, bytes_accessed=4 * (rows + count) * width, transcendentals=0
        ),
        name="pack_pair",
    )(place, tokens, out_grads)


def places(species, expert_table, tensor_size):
    experts = expert_table.shape[0]
    rows_dev = species.shape[0] // tensor_size
    expert_ids = jnp.arange(experts, dtype=jnp.int32)
    species_hits = species == expert_ids[None, :]
    expert_of = jnp.sum(jnp.where(species_hits, expert_table[None, :], 0), axis=1).reshape(
        tensor_size, rows_dev
    )
    onehot = (expert_of[:, :, None] == expert_ids[None, None, :]).astype(jnp.int32)
    earlier = jnp.cumsum(onehot, axis=1) - onehot
    slot_of = jnp.sum(earlier * onehot, axis=2)
    return expert_of, slot_of


def in_pieces(tokens, out_grads, species, expert_table, gate_weight, up_weight, down_weight):
    rows_dev, width = tokens.shape
    experts = expert_table.shape[0]
    depth = 2 * rows_dev // experts // PIECES
    count = experts * depth
    place_of, packed = pack_first(species, expert_table, tokens, out_grads, depth, PIECES)
    exchange = functools.partial(
        lax.all_to_all,
        axis_name="expert",
        split_axis=0,
        concat_axis=0,
        axis_index_groups=[sorted(range(experts), key=lambda i: turn_of(i, experts))],
        tiled=True,
    )
    arrived = [exchange(packed.reshape(experts, depth, 2 * width))]
    for piece in range(1, PIECES):
        packed = pack_pair(place_of, piece, tokens, out_grads, count)
        arrived.append(exchange(packed.reshape(experts, depth, 2 * width)))
    own = None
    for piece in range(PIECES):
        pair = arrived[piece].reshape(count, 2 * width)
        partial_sum = expert_piece(pair, gate_weight, up_weight, down_weight)
        returned = exchange(partial_sum.reshape(experts, depth, width)).reshape(count, width)
        ids = jnp.arange(count, dtype=jnp.int32)
        select = (ids[:, None] == place_of[piece][None, :]).astype(jnp.bfloat16)
        term = dot(select, returned, ((0,), (0,)))
        own = term if own is None else own + term
    return own.astype(jnp.bfloat16)


def in_groups(tokens, out_grads, species, expert_table, gate_weight, up_weight, down_weight):
    tensor_size = lax.axis_size("tensor")
    tensor_index = lax.axis_index("tensor")
    experts = expert_table.shape[0]
    rows_dev = tokens.shape[0] // tensor_size
    model_width = tokens.shape[1] * tensor_size
    capacity = 2 * rows_dev // experts
    expert_of, slot_of = places(species, expert_table, tensor_size)
    group_tokens, group_grads = (
        lax.all_gather(tokens, "tensor", axis=1, tiled=True),
        lax.all_gather(out_grads, "tensor", axis=1, tiled=True),
    )
    place_of = expert_of * capacity + slot_of
    place_ids = jnp.arange(experts * capacity, dtype=jnp.int32)
    select = (place_ids[None, :, None] == place_of[:, None, :]).astype(jnp.bfloat16)

    def send(rows):
        packed = jnp.einsum(
            "tecr,trd->etcd",
            select.reshape(tensor_size, experts, capacity, rows_dev),
            rows.reshape(tensor_size, rows_dev, model_width),
            preferred_element_type=jnp.float32,
        ).astype(jnp.bfloat16)
        packed = packed.reshape(experts, tensor_size * capacity, model_width)
        arrived = lax.all_to_all(packed, "expert", split_axis=0, concat_axis=0, tiled=True)
        return arrived.reshape(-1, model_width)

    partial_sum = expert_partial(
        send(group_tokens), send(group_grads), gate_weight[0], up_weight[0], down_weight[0]
    )
    summed = lax.psum_scatter(
        partial_sum.reshape(experts, tensor_size * capacity, model_width),
        "tensor",
        scatter_dimension=1,
        tiled=True,
    )
    returned = lax.all_to_all(summed, "expert", split_axis=0, concat_axis=0, tiled=True)
    own_select = lax.dynamic_index_in_dim(select, tensor_index, 0, keepdims=False)
    own = dot(own_select, returned.reshape(experts * capacity, model_width), ((0,), (0,)))
    return lax.all_to_all(
        own.astype(jnp.bfloat16), "tensor", split_axis=1, concat_axis=0, tiled=True
    )


def per_device(tokens, out_grads, species, expert_table, *weights):
    whole = lax.axis_size("tensor") == 1
    capacity = 2 * tokens.shape[0] // expert_table.shape[0]
    whole = whole and expert_table.shape[0] % 4 == 0
    form = in_pieces if whole and capacity % (8 * PIECES) == 0 else in_groups
    return form(tokens, out_grads, species, expert_table, *weights)


def solution(mesh):
    placed = (
        P("expert", "tensor"),
        P("expert", "tensor"),
        P("expert", None),
        P(),
        P("expert", None, "tensor"),
        P("expert", None, "tensor"),
        P("expert", "tensor", None),
    )
    return jax.shard_map(
        per_device, mesh=mesh, in_specs=placed, out_specs=P("expert", "tensor"), check_vma=False
    )
```

```python
import functools

import jax
import jax.numpy as jnp
from jax import lax
from jax.experimental import pallas as pl
from jax.experimental.pallas import tpu as pltpu
from jax.sharding import PartitionSpec as P

PIECES = 2
MIB = 1 << 20


def dot(a, b, contract):
    return lax.dot_general(a, b, (contract, ((), ())), preferred_element_type=jnp.float32)


def hidden_grads(gate_pre, up_pre, hidden_grad):
    sigmoid_gate = jax.nn.sigmoid(gate_pre)
    up_grad = (hidden_grad * gate_pre * sigmoid_gate).astype(jnp.bfloat16)
    gate_grad = (
        hidden_grad * up_pre * sigmoid_gate * (1.0 + gate_pre * (1.0 - sigmoid_gate))
    ).astype(jnp.bfloat16)
    return gate_grad, up_grad


def expert_partial(rows, grads, gate, up, down):
    gate_pre, up_pre = dot(rows, gate, ((1,), (0,))), dot(rows, up, ((1,), (0,)))
    hidden_grad = dot(grads, down, ((1,), (1,)))
    gate_grad, up_grad = hidden_grads(gate_pre, up_pre, hidden_grad)
    partial_sum = dot(gate_grad, gate, ((1,), (1,))) + dot(up_grad, up, ((1,), (1,)))
    return partial_sum.astype(jnp.bfloat16)


def expert_kernel(
    pair_ref, gate_ref, up_ref, down_ref, out_ref, wide, tall, even, odd, total, wide_sems, tall_sems
):
    width, tile = out_ref.shape[1], tall.shape[1]
    steps = gate_ref.shape[2] // tile
    half, strip = min(256, tile), min(512, width)
    slots = wide.shape[0]

    def copies(step):
        part = pl.ds(pl.multiple_of(step * tile, tile), tile)
        slot, other = lax.rem(step, slots), lax.rem(step, 2)
        return (
            pltpu.make_async_copy(
                gate_ref.at[0, :, part], wide.at[slot, :, :tile], wide_sems.at[slot, 0]
            ),
            pltpu.make_async_copy(
                up_ref.at[0, :, part], wide.at[slot, :, tile:], wide_sems.at[slot, 1]
            ),
            pltpu.make_async_copy(down_ref.at[0, part, :], tall.at[other], tall_sems.at[other]),
        )

    def first_stage(step, both):
        slot, other = lax.rem(step, slots), lax.rem(step, 2)
        rows, grads = pair_ref[:, :width], pair_ref[:, width:]
        for low in range(0, tile, half):
            high = low + half
            gate_pre = dot(rows, wide[slot, :, low:high], ((1,), (0,)))
            up_pre = dot(rows, wide[slot, :, tile + low : tile + high], ((1,), (0,)))
            hidden_grad = dot(grads, tall[other, low:high, :], ((1,), (1,)))
            gate_grad, up_grad = hidden_grads(gate_pre, up_pre, hidden_grad)
            both[:, low:high] = gate_grad
            both[:, tile + low : tile + high] = up_grad

    def partial_sum(step, both, low):
        slot = lax.rem(step, slots)
        return dot(both[...], wide[slot, low : low + strip, :], ((1,), (1,)))

    def start(step):
        for copy in copies(step):
            copy.start()

    def wait(step):
        for copy in copies(step):
            copy.wait()

    start(0)
    total[...] = jnp.zeros_like(total)
    wait(0)
    if steps > 1:
        start(1)
    first_stage(0, even)

    def skewed(step, now, before):
        wait(step)

        @pl.when(step + 1 < steps)
        def _():
            start(step + 1)

        first_stage(step, now)
        for low in range(0, width, strip):
            total[:, low : low + strip] += partial_sum(step - 1, before, low)

    def body(turn, carry):
        skewed(2 * turn + 1, odd, even)
        skewed(2 * turn + 2, even, odd)
        return carry

    lax.fori_loop(0, (steps - 1) // 2, body, 0)
    if steps % 2 == 0:
        skewed(steps - 1, odd, even)
    last = odd if steps % 2 == 0 else even
    for low in range(0, width, strip):
        high = low + strip
        found = total[:, low:high] + partial_sum(steps - 1, last, low)
        out_ref[:, low:high] = found.astype(out_ref.dtype)


def expert_piece(pair, gate_weight, up_weight, down_weight):
    rows, width = pair.shape[0], pair.shape[1] // 2
    hidden = gate_weight.shape[2]
    tile = min(512, hidden)
    return pl.pallas_call(
        expert_kernel,
        in_specs=[pl.BlockSpec(memory_space=pltpu.VMEM)] + [pl.BlockSpec(memory_space=pl.ANY)] * 3,
        out_specs=pl.BlockSpec(memory_space=pltpu.VMEM),
        out_shape=jax.ShapeDtypeStruct((rows, width), jnp.bfloat16),
        scratch_shapes=[
            pltpu.VMEM((3, width, 2 * tile), jnp.bfloat16),
            pltpu.VMEM((2, tile, width), jnp.bfloat16),
            pltpu.VMEM((rows, 2 * tile), jnp.bfloat16),
            pltpu.VMEM((rows, 2 * tile), jnp.bfloat16),
            pltpu.VMEM((rows, width), jnp.float32),
            pltpu.SemaphoreType.DMA((3, 2)),
            pltpu.SemaphoreType.DMA((2,)),
        ],
        compiler_params=pltpu.CompilerParams(vmem_limit_bytes=40 * MIB),
        cost_estimate=pl.CostEstimate(
            flops=10 * rows * width * hidden,
            bytes_accessed=6 * width * hidden + 6 * rows * width,
            transcendentals=rows * hidden,
        ),
        name="expert_piece",
    )(pair, gate_weight, up_weight, down_weight)


def place_rows(species, table, depth, pieces):
    experts, rows = table.shape[1], species.shape[1]
    ids = lax.broadcasted_iota(jnp.int32, (experts, rows), 0)
    named = (ids == species).astype(jnp.bfloat16)
    expert_ids = lax.broadcasted_iota(jnp.int32, (experts, experts), 0)
    moved = (expert_ids == table).astype(jnp.bfloat16)
    hits = dot(moved, named, ((1,), (0,)))
    row_ids = lax.broadcasted_iota(jnp.int32, (rows, rows), 0)
    column_ids = lax.broadcasted_iota(jnp.int32, (rows, rows), 1)
    before = (row_ids < column_ids).astype(jnp.bfloat16)
    earlier = dot(hits.astype(jnp.bfloat16), before, ((1,), (0,)))
    slot = jnp.sum(earlier * hits, axis=0, keepdims=True).astype(jnp.int32)
    expert = jnp.sum(ids.astype(jnp.float32) * hits, axis=0, keepdims=True).astype(jnp.int32)
    found = []
    for piece in range(pieces):
        own = slot - piece * depth
        found.append(jnp.where((own >= 0) & (own < depth), expert * depth + own, -1))
    return found


def select_rows(place, count):
    ids = lax.broadcasted_iota(jnp.int32, (count, place.shape[1]), 0)
    return (ids == place).astype(jnp.bfloat16)


def first_kernel(
    depth, species_ref, table_ref, rows_ref, grads_ref, place_ref, out_ref, held, packed, sems
):
    width, part = rows_ref.shape[1], held.shape[2]
    parts = width // part
    sources = [ref.at[:, c * part : (c + 1) * part] for ref in (rows_ref, grads_ref) for c in range(parts)]
    arriving = [
        pltpu.make_async_copy(source, held.at[i], sems.at[0, i]) for i, source in enumerate(sources)
    ]
    leaving = [
        pltpu.make_async_copy(packed.at[i], out_ref.at[:, i * part : (i + 1) * part], sems.at[1, i])
        for i in range(2 * parts)
    ]
    for copy in arriving:
        copy.start()
    place = place_rows(species_ref[...], table_ref[...], depth, place_ref.shape[0])
    for piece, found in enumerate(place):
        place_ref[piece : piece + 1, :] = found
    select = select_rows(place[0], packed.shape[1])
    for i in range(2 * parts):
        arriving[i].wait()
        packed[i] = dot(select, held[i], ((1,), (0,))).astype(packed.dtype)
        leaving[i].start()
    for copy in leaving:
        copy.wait()


def pack_first(species, expert_table, tokens, out_grads, depth, pieces):
    (rows, width), experts = tokens.shape, expert_table.shape[0]
    count, part = experts * depth, min(512, width)
    copies = 2 * width // part
    return pl.pallas_call(
        functools.partial(first_kernel, depth),
        in_specs=[pl.BlockSpec(memory_space=pltpu.VMEM)] * 2 + [pl.BlockSpec(memory_space=pl.ANY)] * 2,
        out_specs=[pl.BlockSpec(memory_space=pltpu.VMEM), pl.BlockSpec(memory_space=pl.ANY)],
        out_shape=[
            jax.ShapeDtypeStruct((pieces, rows), jnp.int32),
            jax.ShapeDtypeStruct((count, 2 * width), jnp.bfloat16),
        ],
        scratch_shapes=[
            pltpu.VMEM((copies, rows, part), jnp.bfloat16),
            pltpu.VMEM((copies, count, part), jnp.bfloat16),
            pltpu.SemaphoreType.DMA((2, copies)),
        ],
        compiler_params=pltpu.CompilerParams(vmem_limit_bytes=60 * MIB),
        name="pack_first",
    )(species.reshape(1, rows), expert_table.reshape(1, experts), tokens, out_grads)


def pack_kernel(piece, place_ref, rows_ref, grads_ref, out_ref):
    count, width = out_ref.shape[0], rows_ref.shape[1]
    select = select_rows(place_ref[piece : piece + 1, :], count)
    out_ref[:, :width] = dot(select, rows_ref[...], ((1,), (0,))).astype(out_ref.dtype)
    out_ref[:, width:] = dot(select, grads_ref[...], ((1,), (0,))).astype(out_ref.dtype)


def pack_pair(place, piece, tokens, out_grads, count):
    rows, width = tokens.shape
    return pl.pallas_call(
        functools.partial(pack_kernel, piece),
        out_shape=jax.ShapeDtypeStruct((count, 2 * width), jnp.bfloat16),
        compiler_params=pltpu.CompilerParams(vmem_limit_bytes=24 * MIB),
        cost_estimate=pl.CostEstimate(
            flops=4 * count * rows * width, bytes_accessed=4 * (rows + count) * width, transcendentals=0
        ),
        name="pack_pair",
    )(place, tokens, out_grads)


def places(species, expert_table, tensor_size):
    experts = expert_table.shape[0]
    rows_dev = species.shape[0] // tensor_size
    expert_ids = jnp.arange(experts, dtype=jnp.int32)
    species_hits = species == expert_ids[None, :]
    expert_of = jnp.sum(jnp.where(species_hits, expert_table[None, :], 0), axis=1).reshape(
        tensor_size, rows_dev
    )
    onehot = (expert_of[:, :, None] == expert_ids[None, None, :]).astype(jnp.int32)
    earlier = jnp.cumsum(onehot, axis=1) - onehot
    slot_of = jnp.sum(earlier * onehot, axis=2)
    return expert_of, slot_of


def in_pieces(tokens, out_grads, species, expert_table, gate_weight, up_weight, down_weight):
    rows_dev, width = tokens.shape
    experts = expert_table.shape[0]
    depth = 2 * rows_dev // experts // PIECES
    count = experts * depth
    place_of, packed = pack_first(species, expert_table, tokens, out_grads, depth, PIECES)
    exchange = functools.partial(
        lax.all_to_all, axis_name="expert", split_axis=0, concat_axis=0, tiled=True
    )
    arrived = [exchange(packed.reshape(experts, depth, 2 * width))]
    for piece in range(1, PIECES):
        packed = pack_pair(place_of, piece, tokens, out_grads, count)
        arrived.append(exchange(packed.reshape(experts, depth, 2 * width)))
    own = None
    for piece in range(PIECES):
        pair = arrived[piece].reshape(count, 2 * width)
        partial_sum = expert_piece(pair, gate_weight, up_weight, down_weight)
        returned = exchange(partial_sum.reshape(experts, depth, width)).reshape(count, width)
        ids = jnp.arange(count, dtype=jnp.int32)
        select = (ids[:, None] == place_of[piece][None, :]).astype(jnp.bfloat16)
        term = dot(select, returned, ((0,), (0,)))
        own = term if own is None else own + term
    return own.astype(jnp.bfloat16)


def in_groups(tokens, out_grads, species, expert_table, gate_weight, up_weight, down_weight):
    tensor_size = lax.axis_size("tensor")
    tensor_index = lax.axis_index("tensor")
    experts = expert_table.shape[0]
    rows_dev = tokens.shape[0] // tensor_size
    model_width = tokens.shape[1] * tensor_size
    capacity = 2 * rows_dev // experts
    expert_of, slot_of = places(species, expert_table, tensor_size)
    group_tokens, group_grads = (
        lax.all_gather(tokens, "tensor", axis=1, tiled=True),
        lax.all_gather(out_grads, "tensor", axis=1, tiled=True),
    )
    place_of = expert_of * capacity + slot_of
    place_ids = jnp.arange(experts * capacity, dtype=jnp.int32)
    select = (place_ids[None, :, None] == place_of[:, None, :]).astype(jnp.bfloat16)

    def send(rows):
        packed = jnp.einsum(
            "tecr,trd->etcd",
            select.reshape(tensor_size, experts, capacity, rows_dev),
            rows.reshape(tensor_size, rows_dev, model_width),
            preferred_element_type=jnp.float32,
        ).astype(jnp.bfloat16)
        packed = packed.reshape(experts, tensor_size * capacity, model_width)
        arrived = lax.all_to_all(packed, "expert", split_axis=0, concat_axis=0, tiled=True)
        return arrived.reshape(-1, model_width)

    partial_sum = expert_partial(
        send(group_tokens), send(group_grads), gate_weight[0], up_weight[0], down_weight[0]
    )
    summed = lax.psum_scatter(
        partial_sum.reshape(experts, tensor_size * capacity, model_width),
        "tensor",
        scatter_dimension=1,
        tiled=True,
    )
    returned = lax.all_to_all(summed, "expert", split_axis=0, concat_axis=0, tiled=True)
    own_select = lax.dynamic_index_in_dim(select, tensor_index, 0, keepdims=False)
    own = dot(own_select, returned.reshape(experts * capacity, model_width), ((0,), (0,)))
    return lax.all_to_all(
        own.astype(jnp.bfloat16), "tensor", split_axis=1, concat_axis=0, tiled=True
    )


def per_device(tokens, out_grads, species, expert_table, *weights):
    whole = lax.axis_size("tensor") == 1
    capacity = 2 * tokens.shape[0] // expert_table.shape[0]
    form = in_pieces if whole and capacity % (8 * PIECES) == 0 else in_groups
    return form(tokens, out_grads, species, expert_table, *weights)


def solution(mesh):
    placed = (
        P("expert", "tensor"),
        P("expert", "tensor"),
        P("expert", None),
        P(),
        P("expert", None, "tensor"),
        P("expert", None, "tensor"),
        P("expert", "tensor", None),
    )
    return jax.shard_map(
        per_device, mesh=mesh, in_specs=placed, out_specs=P("expert", "tensor"), check_vma=False
    )
```

```python
import functools

import jax
import jax.numpy as jnp
from jax import lax
from jax.experimental import pallas as pl
from jax.experimental.pallas import tpu as pltpu
from jax.sharding import PartitionSpec as P

PIECES = 2
MIB = 1 << 20


def dot(a, b, contract):
    return lax.dot_general(a, b, (contract, ((), ())), preferred_element_type=jnp.float32)


def hidden_grads(gate_pre, up_pre, hidden_grad):
    sigmoid_gate = jax.nn.sigmoid(gate_pre)
    up_grad = (hidden_grad * gate_pre * sigmoid_gate).astype(jnp.bfloat16)
    gate_grad = (
        hidden_grad * up_pre * sigmoid_gate * (1.0 + gate_pre * (1.0 - sigmoid_gate))
    ).astype(jnp.bfloat16)
    return gate_grad, up_grad


def expert_partial(rows, grads, gate, up, down):
    gate_pre, up_pre = dot(rows, gate, ((1,), (0,))), dot(rows, up, ((1,), (0,)))
    hidden_grad = dot(grads, down, ((1,), (1,)))
    gate_grad, up_grad = hidden_grads(gate_pre, up_pre, hidden_grad)
    partial_sum = dot(gate_grad, gate, ((1,), (1,))) + dot(up_grad, up, ((1,), (1,)))
    return partial_sum.astype(jnp.bfloat16)


def expert_kernel(
    pair_ref, gate_ref, up_ref, down_ref, out_ref, wide, tall, both, total, sems
):
    width, tile = out_ref.shape[1], tall.shape[1]
    steps = gate_ref.shape[2] // tile
    half, strip = min(256, tile), min(512, width)

    def copies(step, slot):
        part = pl.ds(pl.multiple_of(step * tile, tile), tile)
        return [
            pltpu.make_async_copy(source, target, sems.at[slot, i])
            for i, (source, target) in enumerate(
                (
                    (gate_ref.at[0, :, part], wide.at[slot, :, :tile]),
                    (up_ref.at[0, :, part], wide.at[slot, :, tile:]),
                    (down_ref.at[0, part, :], tall.at[slot]),
                )
            )
        ]

    for copy in copies(0, 0):
        copy.start()
    total[...] = jnp.zeros_like(total)

    def body(step, carry):
        slot = lax.rem(step, 2)

        @pl.when(step + 1 < steps)
        def _():
            for copy in copies(step + 1, 1 - slot):
                copy.start()

        for copy in copies(step, slot):
            copy.wait()
        rows, grads = pair_ref[:, :width], pair_ref[:, width:]
        for low in range(0, tile, half):
            high = low + half
            gate_pre = dot(rows, wide[slot, :, low:high], ((1,), (0,)))
            up_pre = dot(rows, wide[slot, :, tile + low : tile + high], ((1,), (0,)))
            hidden_grad = dot(grads, tall[slot, low:high, :], ((1,), (1,)))
            gate_grad, up_grad = hidden_grads(gate_pre, up_pre, hidden_grad)
            both[:, low:high] = gate_grad
            both[:, tile + low : tile + high] = up_grad
        for low in range(0, width, strip):
            high = low + strip
            total[:, low:high] += dot(both[...], wide[slot, low:high, :], ((1,), (1,)))
        return carry

    lax.fori_loop(0, steps, body, 0)
    out_ref[...] = total[...].astype(out_ref.dtype)


def expert_piece(pair, gate_weight, up_weight, down_weight):
    rows, width = pair.shape[0], pair.shape[1] // 2
    hidden = gate_weight.shape[2]
    tile = min(512, hidden)
    return pl.pallas_call(
        expert_kernel,
        in_specs=[pl.BlockSpec(memory_space=pltpu.VMEM)] + [pl.BlockSpec(memory_space=pl.ANY)] * 3,
        out_specs=pl.BlockSpec(memory_space=pltpu.VMEM),
        out_shape=jax.ShapeDtypeStruct((rows, width), jnp.bfloat16),
        scratch_shapes=[
            pltpu.VMEM((2, width, 2 * tile), jnp.bfloat16),
            pltpu.VMEM((2, tile, width), jnp.bfloat16),
            pltpu.VMEM((rows, 2 * tile), jnp.bfloat16),
            pltpu.VMEM((rows, width), jnp.float32),
            pltpu.SemaphoreType.DMA((2, 3)),
        ],
        compiler_params=pltpu.CompilerParams(vmem_limit_bytes=40 * MIB),
        cost_estimate=pl.CostEstimate(
            flops=10 * rows * width * hidden,
            bytes_accessed=6 * width * hidden + 6 * rows * width,
            transcendentals=rows * hidden,
        ),
        name="expert_piece",
    )(pair, gate_weight, up_weight, down_weight)


def place_rows(species, table, depth, pieces):
    experts, rows = table.shape[1], species.shape[1]
    ids = lax.broadcasted_iota(jnp.int32, (experts, rows), 0)
    named = (ids == species).astype(jnp.bfloat16)
    expert_ids = lax.broadcasted_iota(jnp.int32, (experts, experts), 0)
    moved = (expert_ids == table).astype(jnp.bfloat16)
    hits = dot(moved, named, ((1,), (0,)))
    row_ids = lax.broadcasted_iota(jnp.int32, (rows, rows), 0)
    column_ids = lax.broadcasted_iota(jnp.int32, (rows, rows), 1)
    before = (row_ids < column_ids).astype(jnp.bfloat16)
    earlier = dot(hits.astype(jnp.bfloat16), before, ((1,), (0,)))
    slot = jnp.sum(earlier * hits, axis=0, keepdims=True).astype(jnp.int32)
    expert = jnp.sum(ids.astype(jnp.float32) * hits, axis=0, keepdims=True).astype(jnp.int32)
    found = []
    for piece in range(pieces):
        own = slot - piece * depth
        found.append(jnp.where((own >= 0) & (own < depth), expert * depth + own, -1))
    return found


def select_rows(place, count):
    ids = lax.broadcasted_iota(jnp.int32, (count, place.shape[1]), 0)
    return (ids == place).astype(jnp.bfloat16)


def first_kernel(
    depth, species_ref, table_ref, rows_ref, grads_ref, place_ref, out_ref, *scratch
):
    species, table, places_held, held, packed, sems, small_sems = scratch
    width, part = rows_ref.shape[1], held.shape[2]
    parts = width // part
    sources = [ref.at[:, c * part : (c + 1) * part] for ref in (rows_ref, grads_ref) for c in range(parts)]
    arriving = [
        pltpu.make_async_copy(source, held.at[i], sems.at[0, i]) for i, source in enumerate(sources)
    ]
    leaving = [
        pltpu.make_async_copy(packed.at[i], out_ref.at[:, i * part : (i + 1) * part], sems.at[1, i])
        for i in range(2 * parts)
    ]
    named = [
        pltpu.make_async_copy(source, target, small_sems.at[i])
        for i, (source, target) in enumerate(((species_ref, species), (table_ref, table)))
    ]
    for copy in named + arriving:
        copy.start()
    for copy in named:
        copy.wait()
    place = place_rows(species[...], table[...], depth, place_ref.shape[0])
    for piece, found in enumerate(place):
        places_held[piece : piece + 1, :] = found
    placed = pltpu.make_async_copy(places_held, place_ref, small_sems.at[2])
    placed.start()
    select = select_rows(place[0], packed.shape[1])
    for i in range(2 * parts):
        arriving[i].wait()
        packed[i] = dot(select, held[i], ((1,), (0,))).astype(packed.dtype)
        leaving[i].start()
    placed.wait()
    for copy in leaving:
        copy.wait()


def pack_first(species, expert_table, tokens, out_grads, depth, pieces):
    (rows, width), experts = tokens.shape, expert_table.shape[0]
    count, part = experts * depth, min(512, width)
    copies = 2 * width // part
    return pl.pallas_call(
        functools.partial(first_kernel, depth),
        in_specs=[pl.BlockSpec(memory_space=pl.ANY)] * 4,
        out_specs=[pl.BlockSpec(memory_space=pl.ANY)] * 2,
        out_shape=[
            jax.ShapeDtypeStruct((pieces, rows), jnp.int32),
            jax.ShapeDtypeStruct((count, 2 * width), jnp.bfloat16),
        ],
        scratch_shapes=[
            pltpu.VMEM((1, rows), jnp.int32),
            pltpu.VMEM((1, experts), jnp.int32),
            pltpu.VMEM((pieces, rows), jnp.int32),
            pltpu.VMEM((copies, rows, part), jnp.bfloat16),
            pltpu.VMEM((copies, count, part), jnp.bfloat16),
            pltpu.SemaphoreType.DMA((2, copies)),
            pltpu.SemaphoreType.DMA((3,)),
        ],
        compiler_params=pltpu.CompilerParams(vmem_limit_bytes=60 * MIB),
        name="pack_first",
    )(species.reshape(1, rows), expert_table.reshape(1, experts), tokens, out_grads)


def pack_kernel(piece, place_ref, rows_ref, grads_ref, out_ref):
    count, width = out_ref.shape[0], rows_ref.shape[1]
    select = select_rows(place_ref[piece : piece + 1, :], count)
    out_ref[:, :width] = dot(select, rows_ref[...], ((1,), (0,))).astype(out_ref.dtype)
    out_ref[:, width:] = dot(select, grads_ref[...], ((1,), (0,))).astype(out_ref.dtype)


def pack_pair(place, piece, tokens, out_grads, count):
    rows, width = tokens.shape
    return pl.pallas_call(
        functools.partial(pack_kernel, piece),
        out_shape=jax.ShapeDtypeStruct((count, 2 * width), jnp.bfloat16),
        compiler_params=pltpu.CompilerParams(vmem_limit_bytes=24 * MIB),
        cost_estimate=pl.CostEstimate(
            flops=4 * count * rows * width, bytes_accessed=4 * (rows + count) * width, transcendentals=0
        ),
        name="pack_pair",
    )(place, tokens, out_grads)


def places(species, expert_table, tensor_size):
    experts = expert_table.shape[0]
    rows_dev = species.shape[0] // tensor_size
    expert_ids = jnp.arange(experts, dtype=jnp.int32)
    species_hits = species == expert_ids[None, :]
    expert_of = jnp.sum(jnp.where(species_hits, expert_table[None, :], 0), axis=1).reshape(
        tensor_size, rows_dev
    )
    onehot = (expert_of[:, :, None] == expert_ids[None, None, :]).astype(jnp.int32)
    earlier = jnp.cumsum(onehot, axis=1) - onehot
    slot_of = jnp.sum(earlier * onehot, axis=2)
    return expert_of, slot_of


def in_pieces(tokens, out_grads, species, expert_table, gate_weight, up_weight, down_weight):
    rows_dev, width = tokens.shape
    experts = expert_table.shape[0]
    depth = 2 * rows_dev // experts // PIECES
    count = experts * depth
    place_of, packed = pack_first(species, expert_table, tokens, out_grads, depth, PIECES)
    exchange = functools.partial(
        lax.all_to_all, axis_name="expert", split_axis=0, concat_axis=0, tiled=True
    )
    arrived = [exchange(packed.reshape(experts, depth, 2 * width))]
    for piece in range(1, PIECES):
        packed = pack_pair(place_of, piece, tokens, out_grads, count)
        arrived.append(exchange(packed.reshape(experts, depth, 2 * width)))
    own = None
    for piece in range(PIECES):
        pair = arrived[piece].reshape(count, 2 * width)
        partial_sum = expert_piece(pair, gate_weight, up_weight, down_weight)
        returned = exchange(partial_sum.reshape(experts, depth, width)).reshape(count, width)
        ids = jnp.arange(count, dtype=jnp.int32)
        select = (ids[:, None] == place_of[piece][None, :]).astype(jnp.bfloat16)
        term = dot(select, returned, ((0,), (0,)))
        own = term if own is None else own + term
    return own.astype(jnp.bfloat16)


def in_groups(tokens, out_grads, species, expert_table, gate_weight, up_weight, down_weight):
    tensor_size = lax.axis_size("tensor")
    tensor_index = lax.axis_index("tensor")
    experts = expert_table.shape[0]
    rows_dev = tokens.shape[0] // tensor_size
    model_width = tokens.shape[1] * tensor_size
    capacity = 2 * rows_dev // experts
    expert_of, slot_of = places(species, expert_table, tensor_size)
    group_tokens, group_grads = (
        lax.all_gather(tokens, "tensor", axis=1, tiled=True),
        lax.all_gather(out_grads, "tensor", axis=1, tiled=True),
    )
    place_of = expert_of * capacity + slot_of
    place_ids = jnp.arange(experts * capacity, dtype=jnp.int32)
    select = (place_ids[None, :, None] == place_of[:, None, :]).astype(jnp.bfloat16)

    def send(rows):
        packed = jnp.einsum(
            "tecr,trd->etcd",
            select.reshape(tensor_size, experts, capacity, rows_dev),
            rows.reshape(tensor_size, rows_dev, model_width),
            preferred_element_type=jnp.float32,
        ).astype(jnp.bfloat16)
        packed = packed.reshape(experts, tensor_size * capacity, model_width)
        arrived = lax.all_to_all(packed, "expert", split_axis=0, concat_axis=0, tiled=True)
        return arrived.reshape(-1, model_width)

    partial_sum = expert_partial(
        send(group_tokens), send(group_grads), gate_weight[0], up_weight[0], down_weight[0]
    )
    summed = lax.psum_scatter(
        partial_sum.reshape(experts, tensor_size * capacity, model_width),
        "tensor",
        scatter_dimension=1,
        tiled=True,
    )
    returned = lax.all_to_all(summed, "expert", split_axis=0, concat_axis=0, tiled=True)
    own_select = lax.dynamic_index_in_dim(select, tensor_index, 0, keepdims=False)
    own = dot(own_select, returned.reshape(experts * capacity, model_width), ((0,), (0,)))
    return lax.all_to_all(
        own.astype(jnp.bfloat16), "tensor", split_axis=1, concat_axis=0, tiled=True
    )


def per_device(tokens, out_grads, species, expert_table, *weights):
    whole = lax.axis_size("tensor") == 1
    capacity = 2 * tokens.shape[0] // expert_table.shape[0]
    form = in_pieces if whole and capacity % (8 * PIECES) == 0 else in_groups
    return form(tokens, out_grads, species, expert_table, *weights)


def solution(mesh):
    placed = (
        P("expert", "tensor"),
        P("expert", "tensor"),
        P("expert", None),
        P(),
        P("expert", None, "tensor"),
        P("expert", None, "tensor"),
        P("expert", "tensor", None),
    )
    return jax.shard_map(
        per_device, mesh=mesh, in_specs=placed, out_specs=P("expert", "tensor"), check_vma=False
    )
```

```python
import functools

import jax
import jax.numpy as jnp
from jax import lax
from jax.experimental import pallas as pl
from jax.experimental.pallas import tpu as pltpu
from jax.sharding import PartitionSpec as P

PIECES = 2
MIB = 1 << 20


def dot(a, b, contract):
    return lax.dot_general(a, b, (contract, ((), ())), preferred_element_type=jnp.float32)


def hidden_grads(gate_pre, up_pre, hidden_grad):
    sigmoid_gate = jax.nn.sigmoid(gate_pre)
    up_grad = (hidden_grad * gate_pre * sigmoid_gate).astype(jnp.bfloat16)
    gate_grad = (
        hidden_grad * up_pre * sigmoid_gate * (1.0 + gate_pre * (1.0 - sigmoid_gate))
    ).astype(jnp.bfloat16)
    return gate_grad, up_grad


def expert_partial(rows, grads, gate, up, down):
    gate_pre, up_pre = dot(rows, gate, ((1,), (0,))), dot(rows, up, ((1,), (0,)))
    hidden_grad = dot(grads, down, ((1,), (1,)))
    gate_grad, up_grad = hidden_grads(gate_pre, up_pre, hidden_grad)
    partial_sum = dot(gate_grad, gate, ((1,), (1,))) + dot(up_grad, up, ((1,), (1,)))
    return partial_sum.astype(jnp.bfloat16)


def expert_kernel(
    pair_ref, gate_ref, up_ref, down_ref, out_ref, wide, tall, both, total, sems
):
    width, tile = out_ref.shape[1], tall.shape[1]
    steps = gate_ref.shape[2] // tile
    half, strip = min(256, tile), min(512, width)

    def copies(step, slot):
        part = pl.ds(pl.multiple_of(step * tile, tile), tile)
        return [
            pltpu.make_async_copy(source, target, sems.at[slot, i])
            for i, (source, target) in enumerate(
                (
                    (gate_ref.at[0, :, part], wide.at[slot, :, :tile]),
                    (up_ref.at[0, :, part], wide.at[slot, :, tile:]),
                    (down_ref.at[0, part, :], tall.at[slot]),
                )
            )
        ]

    for copy in copies(0, 0):
        copy.start()
    total[...] = jnp.zeros_like(total)

    def body(step, carry):
        slot = lax.rem(step, 2)

        @pl.when(step + 1 < steps)
        def _():
            for copy in copies(step + 1, 1 - slot):
                copy.start()

        gate_copy, up_copy, down_copy = copies(step, slot)
        gate_copy.wait()
        rows, grads = pair_ref[:, :width], pair_ref[:, width:]
        for low in range(0, tile, half):
            high = low + half
            gate_pre = dot(rows, wide[slot, :, low:high], ((1,), (0,)))
            if low == 0:
                up_copy.wait()
            up_pre = dot(rows, wide[slot, :, tile + low : tile + high], ((1,), (0,)))
            if low == 0:
                down_copy.wait()
            hidden_grad = dot(grads, tall[slot, low:high, :], ((1,), (1,)))
            gate_grad, up_grad = hidden_grads(gate_pre, up_pre, hidden_grad)
            both[:, low:high] = gate_grad
            both[:, tile + low : tile + high] = up_grad
        for low in range(0, width, strip):
            high = low + strip
            total[:, low:high] += dot(both[...], wide[slot, low:high, :], ((1,), (1,)))
        return carry

    lax.fori_loop(0, steps, body, 0)
    out_ref[...] = total[...].astype(out_ref.dtype)


def expert_piece(pair, gate_weight, up_weight, down_weight):
    rows, width = pair.shape[0], pair.shape[1] // 2
    hidden = gate_weight.shape[2]
    tile = min(512, hidden)
    return pl.pallas_call(
        expert_kernel,
        in_specs=[pl.BlockSpec(memory_space=pltpu.VMEM)] + [pl.BlockSpec(memory_space=pl.ANY)] * 3,
        out_specs=pl.BlockSpec(memory_space=pltpu.VMEM),
        out_shape=jax.ShapeDtypeStruct((rows, width), jnp.bfloat16),
        scratch_shapes=[
            pltpu.VMEM((2, width, 2 * tile), jnp.bfloat16),
            pltpu.VMEM((2, tile, width), jnp.bfloat16),
            pltpu.VMEM((rows, 2 * tile), jnp.bfloat16),
            pltpu.VMEM((rows, width), jnp.float32),
            pltpu.SemaphoreType.DMA((2, 3)),
        ],
        compiler_params=pltpu.CompilerParams(vmem_limit_bytes=40 * MIB),
        cost_estimate=pl.CostEstimate(
            flops=10 * rows * width * hidden,
            bytes_accessed=6 * width * hidden + 6 * rows * width,
            transcendentals=rows * hidden,
        ),
        name="expert_piece",
    )(pair, gate_weight, up_weight, down_weight)


def place_rows(species, table, depth, pieces):
    experts, rows = table.shape[1], species.shape[1]
    ids = lax.broadcasted_iota(jnp.int32, (experts, rows), 0)
    named = (ids == species).astype(jnp.bfloat16)
    expert_ids = lax.broadcasted_iota(jnp.int32, (experts, experts), 0)
    moved = (expert_ids == table).astype(jnp.bfloat16)
    hits = dot(moved, named, ((1,), (0,)))
    row_ids = lax.broadcasted_iota(jnp.int32, (rows, rows), 0)
    column_ids = lax.broadcasted_iota(jnp.int32, (rows, rows), 1)
    before = (row_ids < column_ids).astype(jnp.bfloat16)
    earlier = dot(hits.astype(jnp.bfloat16), before, ((1,), (0,)))
    slot = jnp.sum(earlier * hits, axis=0, keepdims=True).astype(jnp.int32)
    expert = jnp.sum(ids.astype(jnp.float32) * hits, axis=0, keepdims=True).astype(jnp.int32)
    found = []
    for piece in range(pieces):
        own = slot - piece * depth
        found.append(jnp.where((own >= 0) & (own < depth), expert * depth + own, -1))
    return found


def select_rows(place, count):
    ids = lax.broadcasted_iota(jnp.int32, (count, place.shape[1]), 0)
    return (ids == place).astype(jnp.bfloat16)


def first_kernel(
    depth, species_ref, table_ref, rows_ref, grads_ref, place_ref, out_ref, *scratch
):
    species, table, places_held, held, packed, sems, small_sems = scratch
    width, part = rows_ref.shape[1], held.shape[2]
    parts = width // part
    sources = [ref.at[:, c * part : (c + 1) * part] for ref in (rows_ref, grads_ref) for c in range(parts)]
    arriving = [
        pltpu.make_async_copy(source, held.at[i], sems.at[0, i]) for i, source in enumerate(sources)
    ]
    leaving = [
        pltpu.make_async_copy(packed.at[i], out_ref.at[:, i * part : (i + 1) * part], sems.at[1, i])
        for i in range(2 * parts)
    ]
    named = [
        pltpu.make_async_copy(source, target, small_sems.at[i])
        for i, (source, target) in enumerate(((species_ref, species), (table_ref, table)))
    ]
    for copy in named + arriving:
        copy.start()
    for copy in named:
        copy.wait()
    place = place_rows(species[...], table[...], depth, place_ref.shape[0])
    for piece, found in enumerate(place):
        places_held[piece : piece + 1, :] = found
    placed = pltpu.make_async_copy(places_held, place_ref, small_sems.at[2])
    placed.start()
    select = select_rows(place[0], packed.shape[1])
    for i in range(2 * parts):
        arriving[i].wait()
        packed[i] = dot(select, held[i], ((1,), (0,))).astype(packed.dtype)
        leaving[i].start()
    placed.wait()
    for copy in leaving:
        copy.wait()


def pack_first(species, expert_table, tokens, out_grads, depth, pieces):
    (rows, width), experts = tokens.shape, expert_table.shape[0]
    count, part = experts * depth, min(512, width)
    copies = 2 * width // part
    return pl.pallas_call(
        functools.partial(first_kernel, depth),
        in_specs=[pl.BlockSpec(memory_space=pl.ANY)] * 4,
        out_specs=[pl.BlockSpec(memory_space=pl.ANY)] * 2,
        out_shape=[
            jax.ShapeDtypeStruct((pieces, rows), jnp.int32),
            jax.ShapeDtypeStruct((count, 2 * width), jnp.bfloat16),
        ],
        scratch_shapes=[
            pltpu.VMEM((1, rows), jnp.int32),
            pltpu.VMEM((1, experts), jnp.int32),
            pltpu.VMEM((pieces, rows), jnp.int32),
            pltpu.VMEM((copies, rows, part), jnp.bfloat16),
            pltpu.VMEM((copies, count, part), jnp.bfloat16),
            pltpu.SemaphoreType.DMA((2, copies)),
            pltpu.SemaphoreType.DMA((3,)),
        ],
        compiler_params=pltpu.CompilerParams(vmem_limit_bytes=60 * MIB),
        name="pack_first",
    )(species.reshape(1, rows), expert_table.reshape(1, experts), tokens, out_grads)


def pack_kernel(piece, place_ref, rows_ref, grads_ref, out_ref):
    count, width = out_ref.shape[0], rows_ref.shape[1]
    select = select_rows(place_ref[piece : piece + 1, :], count)
    out_ref[:, :width] = dot(select, rows_ref[...], ((1,), (0,))).astype(out_ref.dtype)
    out_ref[:, width:] = dot(select, grads_ref[...], ((1,), (0,))).astype(out_ref.dtype)


def pack_pair(place, piece, tokens, out_grads, count):
    rows, width = tokens.shape
    return pl.pallas_call(
        functools.partial(pack_kernel, piece),
        out_shape=jax.ShapeDtypeStruct((count, 2 * width), jnp.bfloat16),
        compiler_params=pltpu.CompilerParams(vmem_limit_bytes=24 * MIB),
        cost_estimate=pl.CostEstimate(
            flops=4 * count * rows * width, bytes_accessed=4 * (rows + count) * width, transcendentals=0
        ),
        name="pack_pair",
    )(place, tokens, out_grads)


def places(species, expert_table, tensor_size):
    experts = expert_table.shape[0]
    rows_dev = species.shape[0] // tensor_size
    expert_ids = jnp.arange(experts, dtype=jnp.int32)
    species_hits = species == expert_ids[None, :]
    expert_of = jnp.sum(jnp.where(species_hits, expert_table[None, :], 0), axis=1).reshape(
        tensor_size, rows_dev
    )
    onehot = (expert_of[:, :, None] == expert_ids[None, None, :]).astype(jnp.int32)
    earlier = jnp.cumsum(onehot, axis=1) - onehot
    slot_of = jnp.sum(earlier * onehot, axis=2)
    return expert_of, slot_of


def in_pieces(tokens, out_grads, species, expert_table, gate_weight, up_weight, down_weight):
    rows_dev, width = tokens.shape
    experts = expert_table.shape[0]
    depth = 2 * rows_dev // experts // PIECES
    count = experts * depth
    place_of, packed = pack_first(species, expert_table, tokens, out_grads, depth, PIECES)
    exchange = functools.partial(
        lax.all_to_all, axis_name="expert", split_axis=0, concat_axis=0, tiled=True
    )
    arrived = [exchange(packed.reshape(experts, depth, 2 * width))]
    for piece in range(1, PIECES):
        packed = pack_pair(place_of, piece, tokens, out_grads, count)
        arrived.append(exchange(packed.reshape(experts, depth, 2 * width)))
    own = None
    for piece in range(PIECES):
        pair = arrived[piece].reshape(count, 2 * width)
        partial_sum = expert_piece(pair, gate_weight, up_weight, down_weight)
        returned = exchange(partial_sum.reshape(experts, depth, width)).reshape(count, width)
        ids = jnp.arange(count, dtype=jnp.int32)
        select = (ids[:, None] == place_of[piece][None, :]).astype(jnp.bfloat16)
        term = dot(select, returned, ((0,), (0,)))
        own = term if own is None else own + term
    return own.astype(jnp.bfloat16)


def in_groups(tokens, out_grads, species, expert_table, gate_weight, up_weight, down_weight):
    tensor_size = lax.axis_size("tensor")
    tensor_index = lax.axis_index("tensor")
    experts = expert_table.shape[0]
    rows_dev = tokens.shape[0] // tensor_size
    model_width = tokens.shape[1] * tensor_size
    capacity = 2 * rows_dev // experts
    expert_of, slot_of = places(species, expert_table, tensor_size)
    group_tokens, group_grads = (
        lax.all_gather(tokens, "tensor", axis=1, tiled=True),
        lax.all_gather(out_grads, "tensor", axis=1, tiled=True),
    )
    place_of = expert_of * capacity + slot_of
    place_ids = jnp.arange(experts * capacity, dtype=jnp.int32)
    select = (place_ids[None, :, None] == place_of[:, None, :]).astype(jnp.bfloat16)

    def send(rows):
        packed = jnp.einsum(
            "tecr,trd->etcd",
            select.reshape(tensor_size, experts, capacity, rows_dev),
            rows.reshape(tensor_size, rows_dev, model_width),
            preferred_element_type=jnp.float32,
        ).astype(jnp.bfloat16)
        packed = packed.reshape(experts, tensor_size * capacity, model_width)
        arrived = lax.all_to_all(packed, "expert", split_axis=0, concat_axis=0, tiled=True)
        return arrived.reshape(-1, model_width)

    partial_sum = expert_partial(
        send(group_tokens), send(group_grads), gate_weight[0], up_weight[0], down_weight[0]
    )
    summed = lax.psum_scatter(
        partial_sum.reshape(experts, tensor_size * capacity, model_width),
        "tensor",
        scatter_dimension=1,
        tiled=True,
    )
    returned = lax.all_to_all(summed, "expert", split_axis=0, concat_axis=0, tiled=True)
    own_select = lax.dynamic_index_in_dim(select, tensor_index, 0, keepdims=False)
    own = dot(own_select, returned.reshape(experts * capacity, model_width), ((0,), (0,)))
    return lax.all_to_all(
        own.astype(jnp.bfloat16), "tensor", split_axis=1, concat_axis=0, tiled=True
    )


def per_device(tokens, out_grads, species, expert_table, *weights):
    whole = lax.axis_size("tensor") == 1
    capacity = 2 * tokens.shape[0] // expert_table.shape[0]
    form = in_pieces if whole and capacity % (8 * PIECES) == 0 else in_groups
    return form(tokens, out_grads, species, expert_table, *weights)


def solution(mesh):
    placed = (
        P("expert", "tensor"),
        P("expert", "tensor"),
        P("expert", None),
        P(),
        P("expert", None, "tensor"),
        P("expert", None, "tensor"),
        P("expert", "tensor", None),
    )
    return jax.shard_map(
        per_device, mesh=mesh, in_specs=placed, out_specs=P("expert", "tensor"), check_vma=False
    )
```
